32 devices in a mesh: seg: 4 (over y, core), mic: 8 (over z, x).
Axes of the slice: x: 2, y: 2, z: 4, core: 2. Of those that a mesh axis runs over, the one named last changes fastest.
Arguments:
- time_data: bfloat16 [128, 512, 1024], P('seg', 'mic'), may hold values from -6 to 6
- order_bin: int32 [1], replicated, may hold values from 32 to 203
- mic_pos: int32 [3, 512], replicated, may hold values from -2000 to 2000
- grid_pos: int32 [3, 16384], P(None, 'mic'), may hold values from -1500 to 1500
Outputs:
- beam_power: float32 [8, 2048], P('mic', 'seg')
The draws below stay inside these ranges and needn't reach their ends.
All inputs are finite; a program needn't handle non-finite values.
Results may differ from the reference program's by a relative error of at most 0.00083.
Values may be sent and summed in bfloat16 or wider, within the bound.
No kernel may reach another device: no remote copies, remote signals or barrier semaphores. Data moves between devices by JAX's collectives and lax.ppermute only.
A program may use at most 256 MiB of HBM per device.

```python
import math
import jax
import jax.numpy as jnp
from jax import lax

L = 1024
MIC = 512
SEG = 128
SLAB = 2048
GRID = 16384
N_MIC = 8


def place_ends(array, key, smallest, largest):
    longest = array.shape.index(max(array.shape))
    spots = []
    for shift in (0, 1):
        where = [jax.random.randint(jax.random.fold_in(key, axis), (), 0, length) for axis, length in enumerate(array.shape)]
        where[longest] = (where[longest] + shift) % array.shape[longest]
        spots.append(tuple(where))
    return array.at[spots[0]].set(smallest).at[spots[1]].set(largest)


def levels(own_key, dims, shards, low, high):
    level = 1.0
    for axis_at, parts in shards:
        steps = jax.random.uniform(jax.random.fold_in(jax.random.fold_in(own_key, 6), axis_at), (parts,), jnp.float32, low / len(shards), high / len(shards))
        level = level * jnp.repeat(jnp.exp(steps), dims[axis_at] // parts).reshape((-1,) + (1,) * (len(dims) - 1 - axis_at))
    return level


def normal_values(rng, shape, deviation, reach, cuts=(), held_as=jnp.bfloat16):
    drawn = deviation * jax.random.normal(rng, shape, jnp.float32)
    if cuts:
        drawn = drawn * levels(rng, shape, cuts, -0.22, 0.18)
    return jnp.clip(drawn, -reach, reach).astype(held_as)


def setup_inputs(seed: int = 0) -> dict:
    key_list = jax.random.split(jax.random.key(seed), 5)
    return {
        "time_data": normal_values(key_list[0], (SEG, MIC, L), 1.0, 6.0, ((0, 4), (1, 8))),
        "order_bin": jax.random.randint(key_list[1], (1,), L // 32, L // 5).astype(jnp.int32),
        "mic_pos": place_ends(jax.random.randint(key_list[2], (3, MIC), -2000, 2001), jax.random.fold_in(key_list[2], 1), -2000, 2000).astype(jnp.int32),
        "grid_pos": place_ends(jax.random.randint(key_list[3], (3, GRID), -1500, 1501), jax.random.fold_in(key_list[3], 1), -1500, 1500).astype(jnp.int32),
    }


def spectral_table(order_value, samples):
    times = jnp.arange(samples, dtype=jnp.int32)
    turned = order_value * times % samples
    angle = turned.astype(jnp.float32) * (2.0 * math.pi / samples)
    window = 0.5 - 0.5 * jnp.cos(times.astype(jnp.float32) * (2.0 * math.pi / samples))
    return jnp.stack([window * jnp.cos(angle), -(window * jnp.sin(angle))]).astype(jnp.bfloat16)

def stacked_left(spectra):
    real_part = spectra[0]
    imag_part = spectra[1]
    upper = jnp.concatenate([real_part, -imag_part], axis=1)
    lower = jnp.concatenate([imag_part, real_part], axis=1)
    return jnp.concatenate([upper, lower], axis=0)

def beam_block(left, mic_part, points, wave):
    offsets = (points[:, None, :] - mic_part[:, :, None]).astype(jnp.float32) * 0.001
    distance = jnp.sqrt(offsets[0] * offsets[0] + offsets[1] * offsets[1] + offsets[2] * offsets[2])
    phase = wave * distance
    steering = jnp.concatenate([jnp.cos(phase), jnp.sin(phase)], axis=0).astype(jnp.bfloat16)
    return jnp.dot(left, steering, preferred_element_type=jnp.float32)

def reference(time_data, order_bin, mic_pos, grid_pos):
    table = spectral_table(order_bin[0], L)
    rows = time_data.reshape(SEG * MIC, L)
    spec = jnp.dot(rows, table.T, preferred_element_type=jnp.float32)
    spectra = spec.T.reshape(2, SEG, MIC).astype(jnp.bfloat16)
    wave = order_bin[0].astype(jnp.float32) * jnp.float32(2.0 * math.pi * 51200.0 / 343.0) / jnp.float32(L)
    left = stacked_left(spectra)
    denom = jnp.float32(SEG * MIC * 0.375 * L)
    block = math.gcd(GRID, 512)
    blocks = grid_pos.reshape(3, GRID // block, block).transpose(1, 0, 2)

    def one_block(points):
        beams = beam_block(left, mic_pos, points, wave)
        return lax.optimization_barrier(jnp.sum(beams * beams, axis=0)) / denom
    return lax.map(one_block, blocks).reshape(N_MIC, SLAB)
```

```python
import functools
import math

import jax
import jax.numpy as jnp
import numpy as np
from jax import lax
from jax.experimental import pallas as pl
from jax.experimental.pallas import tpu as pltpu
from jax.sharding import PartitionSpec as P

LANES = 128
VMEM_LIMIT = 60 * 1024 * 1024


def fitted(values, degree):
    count = degree + 1
    nodes = 0.125 + 0.125 * np.cos((2 * np.arange(count) + 1) * np.pi / (2 * count))
    return [float(c) for c in np.linalg.solve(np.vander(nodes, count, increasing=True), values(nodes))]


COS_FIT = fitted(lambda q: np.cos(2 * np.pi * np.sqrt(q)), 6)
SIN_FIT = fitted(lambda q: np.sin(2 * np.pi * np.sqrt(q)) / np.sqrt(q), 6)


def horner(coefficients, q):
    total = jnp.full_like(q, coefficients[-1])
    for c in coefficients[-2::-1]:
        total = total * q + c
    return total


def cos_sin_turns(turns):
    r = turns - jnp.round(turns)
    q = r * r
    return horner(COS_FIT, q), r * horner(SIN_FIT, q)


def spectra_kernel(order_ref, data_ref, out_ref, held, rows_ref, sems, *, chunks):
    seg, mic, samples = held.shape
    part = seg // chunks
    copies = [
        pltpu.make_async_copy(
            data_ref.at[pl.ds(k * part, part)], held.at[pl.ds(k * part, part)], sems.at[k]
        )
        for k in range(chunks)
    ]
    for copy in copies:
        copy.start()
    times = lax.broadcasted_iota(jnp.int32, (16, samples), 1)
    row = lax.broadcasted_iota(jnp.int32, (16, samples), 0)
    turned = lax.rem(order_ref[0] * times, jnp.int32(samples))
    cos_w, _ = cos_sin_turns(times.astype(jnp.float32) * (1.0 / samples))
    cos_a, sin_a = cos_sin_turns(turned.astype(jnp.float32) * (1.0 / samples))
    window = 0.5 - 0.5 * cos_w
    table = jnp.where(row == 0, window * cos_a, jnp.where(row == 1, -(window * sin_a), 0.0))
    table = table.astype(jnp.bfloat16)
    lines = seg * mic // LANES
    per = part * mic // LANES
    for k in range(chunks):
        copies[k].wait()
        block = held[pl.ds(k * part, part)].reshape(part * mic, samples)
        spec = lax.dot_general(
            table, block, (((1,), (1,)), ((), ())), preferred_element_type=jnp.float32
        )
        for j in range(per):
            line = k * per + j
            rows_ref[pl.ds(line, 1), :] = spec[0:1, j * LANES : (j + 1) * LANES]
            rows_ref[pl.ds(lines + line, 1), :] = spec[1:2, j * LANES : (j + 1) * LANES]
    out_ref[...] = rows_ref[...].astype(jnp.bfloat16)


def spectra_of(order_bin, time_data, chunks=4):
    seg, mic, samples = time_data.shape
    lines = seg * mic // LANES
    return pl.pallas_call(
        functools.partial(spectra_kernel, chunks=chunks),
        out_shape=jax.ShapeDtypeStruct((2 * lines, LANES), jnp.bfloat16),
        in_specs=[pl.BlockSpec(memory_space=pltpu.SMEM), pl.BlockSpec(memory_space=pltpu.HBM)],
        out_specs=pl.BlockSpec(memory_space=pltpu.VMEM),
        scratch_shapes=[
            pltpu.VMEM(time_data.shape, time_data.dtype),
            pltpu.VMEM((2 * lines, LANES), jnp.float32),
            pltpu.SemaphoreType.DMA((chunks,)),
        ],
        compiler_params=pltpu.CompilerParams(vmem_limit_bytes=VMEM_LIMIT),
        cost_estimate=pl.CostEstimate(
            flops=4 * time_data.size, bytes_accessed=2 * time_data.size, transcendentals=0
        ),
    )(order_bin, time_data)


def steering_kernel(order_ref, mic_ref, grid_ref, after_ref, out_ref, column, *, masks, samples, width):
    del after_ref
    own_pair = lax.shift_right_logical(lax.axis_index("mic"), 1)
    offset = pl.multiple_of(lax.axis_index("seg") * width, width)
    per_mm = order_ref[0].astype(jnp.float32) * jnp.float32(51200.0 / 343.0 / 1000.0 / samples)
    points = grid_ref[:, pl.ds(offset, width)].astype(jnp.float32)
    for k, mask in enumerate(masks):
        start = pl.multiple_of(lax.bitwise_xor(own_pair, jnp.int32(mask)) * LANES, LANES)
        mics = mic_ref[:, pl.ds(start, LANES)].astype(jnp.float32)
        mics = jnp.concatenate([mics, jnp.zeros((5, LANES), jnp.float32)], axis=0)
        column[...] = jnp.transpose(mics)

        def sixteen(i, carry, k=k):
            first = pl.multiple_of(i * 16, 16)
            mine = column[pl.ds(first, 16), :]
            square = None
            for axis in range(3):
                gap = points[axis : axis + 1, :] - mine[:, axis : axis + 1]
                square = gap * gap if square is None else square + gap * gap
            turns = square * lax.rsqrt(jnp.maximum(square, 1.0)) * per_mm
            cosine, sine = cos_sin_turns(turns)
            out_ref[k, pl.ds(first, 16), :] = cosine.astype(jnp.bfloat16)
            out_ref[k, pl.ds(LANES + first, 16), :] = sine.astype(jnp.bfloat16)
            return carry

        lax.fori_loop(0, LANES // 16, sixteen, 0)


def steering_of(order_bin, mic_pos, grid_pos, after, masks, samples, width):
    return pl.pallas_call(
        functools.partial(steering_kernel, masks=masks, samples=samples, width=width),
        out_shape=jax.ShapeDtypeStruct((len(masks), 2 * LANES, width), jnp.bfloat16),
        in_specs=[pl.BlockSpec(memory_space=pltpu.SMEM)] + [pl.BlockSpec(memory_space=pltpu.VMEM)] * 3,
        out_specs=pl.BlockSpec(memory_space=pltpu.VMEM),
        scratch_shapes=[pltpu.VMEM((LANES, 8), jnp.float32)],
        compiler_params=pltpu.CompilerParams(vmem_limit_bytes=32 * 1024 * 1024),
        cost_estimate=pl.CostEstimate(
            flops=50 * len(masks) * LANES * width, bytes_accessed=4 * len(masks) * LANES * width, transcendentals=0
        ),
    )(order_bin, mic_pos, grid_pos, after)


def left_blocks(own, other, odd):
    pairs, rows, _ = own.shape
    own = own.astype(jnp.float32).reshape(pairs * rows, LANES)
    other = other.astype(jnp.float32).reshape(pairs * rows, LANES)
    lower = jnp.where(odd, other, own)
    upper = jnp.where(odd, own, other)
    half = lax.broadcasted_iota(jnp.int32, lower.shape, 1) < LANES // 2
    even_segs = jnp.where(half, lower, pltpu.roll(upper, LANES // 2, 1))
    odd_segs = jnp.where(half, pltpu.roll(lower, LANES // 2, 1), upper)
    return [x.reshape(pairs, rows, LANES) for x in (even_segs, odd_segs)]


def power_kernel(a_ref, b_ref, c_ref, d_ref, steer_ref, before_ref, out_ref, *, scale):
    odd = lax.bitwise_and(lax.axis_index("mic"), 1) == 1
    pieces = left_blocks(a_ref[...], b_ref[...], odd) + left_blocks(c_ref[...], d_ref[...], odd)
    pairs, rows, _ = a_ref.shape
    lines = rows // 2
    beams = None
    for k in range(pairs):
        left = []
        for piece in pieces:
            x = piece[k]
            turned = jnp.concatenate([-x[lines:], x[:lines]], axis=0)
            left.append(jnp.concatenate([x, turned], axis=1))
        left = jnp.concatenate(left, axis=0).astype(jnp.bfloat16)
        term = jnp.dot(left, steer_ref[k], preferred_element_type=jnp.float32)
        beams = term if beams is None else beams + term
    power = jnp.sum((beams * beams).reshape(-1, 8, beams.shape[1]), axis=0) + before_ref[...]
    if scale is None:
        out_ref[...] = power
    else:
        out_ref[...] = jnp.sum(power, axis=0, keepdims=True) / jnp.float32(scale)


def power_of(blocks, steering, before, scale):
    width = steering.shape[2]
    shape = (8 if scale is None else 1, width)
    pairs, rows, _ = blocks[0].shape
    return pl.pallas_call(
        functools.partial(power_kernel, scale=scale),
        out_shape=jax.ShapeDtypeStruct(shape, jnp.float32),
        in_specs=[pl.BlockSpec(memory_space=pltpu.VMEM)] * 6,
        out_specs=pl.BlockSpec(memory_space=pltpu.VMEM),
        compiler_params=pltpu.CompilerParams(vmem_limit_bytes=32 * 1024 * 1024),
        cost_estimate=pl.CostEstimate(
            flops=2 * 4 * rows * steering.size, bytes_accessed=2 * steering.size, transcendentals=0
        ),
    )(*blocks, steering, before)


def shards(time_data, order_bin, mic_pos, grid_pos):
    seg_dev, mic_dev, samples = time_data.shape
    seg_count = lax.axis_size("seg")
    mic_count = lax.axis_size("mic")
    own_width = grid_pos.shape[1] // seg_count
    denom = seg_count * seg_dev * mic_count * mic_dev * 0.375 * samples

    def swap(x, mask):
        pairs = [(i, i ^ mask) for i in range(seg_count * mic_count)]
        return lax.ppermute(x, ("seg", "mic"), pairs)

    spectra = spectra_of(order_bin, time_data)
    held = spectra[None]
    masks = [0]
    bit = mic_count // 2
    while bit > 1:
        held = jnp.concatenate([held, swap(held, bit)], axis=0)
        masks += [m ^ (bit // 2) for m in masks]
        bit //= 2
    steering = steering_of(order_bin, mic_pos, grid_pos, spectra, masks, samples, own_width)
    far = 2 * mic_count
    both = swap(held, far + 1)
    beside = swap(held, 1)
    across = swap(held, far)
    blocks = [held, beside, across, both]
    twin = swap(jnp.concatenate(blocks, axis=0), mic_count)
    pairs = len(masks)
    twins = [twin[i * pairs : (i + 1) * pairs] for i in range(4)]
    half = power_of(blocks, steering, jnp.zeros((8, own_width), jnp.float32), None)
    return power_of(twins, steering, half, denom)


def solution(mesh):
    placed = (P("seg", "mic", None), P(), P(), P(None, "mic"))
    return jax.shard_map(
        shards, mesh=mesh, in_specs=placed, out_specs=P("mic", "seg"), check_vma=False
    )
```

```python
import functools
import math

import jax
import jax.numpy as jnp
import numpy as np
from jax import lax
from jax.experimental import pallas as pl
from jax.experimental.pallas import tpu as pltpu
from jax.sharding import PartitionSpec as P

LANES = 128
MIB = 1024 * 1024
NEAREST = 1.5 * 2.0**23


def fitted(values, degree):
    count = degree + 1
    nodes = 0.125 + 0.125 * np.cos((2 * np.arange(count) + 1) * np.pi / (2 * count))
    return [float(c) for c in np.linalg.solve(np.vander(nodes, count, increasing=True), values(nodes))]


COS_FIT = fitted(lambda q: np.cos(2 * np.pi * np.sqrt(q)), 6)
SIN_FIT = fitted(lambda q: np.sin(2 * np.pi * np.sqrt(q)) / np.sqrt(q), 5)


def horner(coefficients, q):
    total = q * coefficients[-1] + coefficients[-2]
    for c in coefficients[-3::-1]:
        total = total * q + c
    return total


def cos_sin_turns(turns):
    r = turns - ((turns + NEAREST) - NEAREST)
    q = r * r
    return horner(COS_FIT, q), r * horner(SIN_FIT, q)


def spectra_kernel(order_ref, data_ref, out_ref, scale_ref, held, rows_ref, order_s, sems, order_sem, *, parts):
    seg, mic, samples = held.shape
    starts = [sum(parts[:k]) for k in range(len(parts))]
    copies = [
        pltpu.make_async_copy(data_ref.at[pl.ds(a, n)], held.at[pl.ds(a, n)], sems.at[k])
        for k, (a, n) in enumerate(zip(starts, parts))
    ]
    order_copy = pltpu.make_async_copy(order_ref, order_s, order_sem)
    order_copy.start()
    for copy in copies:
        copy.start()
    times = lax.broadcasted_iota(jnp.int32, (8, samples), 1)
    row = lax.broadcasted_iota(jnp.int32, (8, samples), 0)
    cos_w, _ = cos_sin_turns(times.astype(jnp.float32) * (1.0 / samples))
    window = 0.5 - 0.5 * cos_w
    order_copy.wait()
    order = order_s[0]
    per_mm = order.astype(jnp.float32) * jnp.float32(51200.0 / 343.0 / 1000.0 / samples)
    scale_ref[...] = jnp.full(scale_ref.shape, per_mm)
    turned = lax.rem(order * times, jnp.int32(samples))
    cos_a, sin_a = cos_sin_turns(turned.astype(jnp.float32) * (1.0 / samples))
    table = jnp.where(row == 0, window * cos_a, jnp.where(row == 1, -(window * sin_a), 0.0))
    table = table.astype(jnp.bfloat16)
    lines = seg * mic // LANES
    found = []
    for k, (a, n) in enumerate(zip(starts, parts)):
        copies[k].wait()
        block = held[pl.ds(a, n)].reshape(n * mic, samples)
        spec = lax.dot_general(
            table, block, (((1,), (1,)), ((), ())), preferred_element_type=jnp.float32
        )
        found += [spec[:, j : j + LANES] for j in range(0, n * mic, LANES)]
    for line, spec in enumerate(found):
        rows_ref[pl.ds(line, 1), :] = spec[0:1]
        rows_ref[pl.ds(lines + line, 1), :] = spec[1:2]
    out_ref[...] = rows_ref[...].astype(jnp.bfloat16)


def spectra_of(order_bin, time_data):
    seg, mic, samples = time_data.shape
    lines = seg * mic // LANES
    parts = (seg // 2, seg // 2)
    return pl.pallas_call(
        functools.partial(spectra_kernel, parts=parts),
        out_shape=[
            jax.ShapeDtypeStruct((2 * lines, LANES), jnp.bfloat16),
            jax.ShapeDtypeStruct((8, LANES), jnp.float32),
        ],
        in_specs=[pl.BlockSpec(memory_space=pltpu.HBM)] * 2,
        out_specs=[pl.BlockSpec(memory_space=pltpu.VMEM)] * 2,
        scratch_shapes=[
            pltpu.VMEM(time_data.shape, time_data.dtype),
            pltpu.VMEM((2 * lines, LANES), jnp.float32),
            pltpu.SMEM((1,), jnp.int32),
            pltpu.SemaphoreType.DMA((len(parts),)),
            pltpu.SemaphoreType.DMA,
        ],
        compiler_params=pltpu.CompilerParams(vmem_limit_bytes=51 * MIB),
        cost_estimate=pl.CostEstimate(
            flops=4 * time_data.size, bytes_accessed=2 * time_data.size, transcendentals=0
        ),
    )(order_bin, time_data)


def steering_kernel(scale_ref, mic_ref, grid_ref, out_ref, column, *, masks, width):
    own_pair = lax.shift_right_logical(lax.axis_index("mic"), 1)
    offset = pl.multiple_of(lax.axis_index("seg") * width, width)
    points = grid_ref[:, pl.ds(offset, width)].astype(jnp.float32)
    per_mm = scale_ref[0:1, 0:1]
    for k, mask in enumerate(masks):
        start = pl.multiple_of(lax.bitwise_xor(own_pair, jnp.int32(mask)) * LANES, LANES)
        mics = mic_ref[:, pl.ds(start, LANES)].astype(jnp.float32)
        mics = jnp.concatenate([mics, jnp.zeros((5, LANES), jnp.float32)], axis=0)
        column[...] = jnp.transpose(mics)

        def sixteen(i, carry, k=k):
            first = pl.multiple_of(i * 16, 16)
            mine = column[pl.ds(first, 16), :]
            square = None
            for axis in range(3):
                gap = points[axis : axis + 1, :] - mine[:, axis : axis + 1]
                square = gap * gap if square is None else square + gap * gap
            turns = square * lax.rsqrt(jnp.maximum(square, 1.0)) * per_mm
            cosine, sine = cos_sin_turns(turns)
            out_ref[k, pl.ds(first, 16), :] = cosine.astype(jnp.bfloat16)
            out_ref[k, pl.ds(LANES + first, 16), :] = sine.astype(jnp.bfloat16)
            return carry

        lax.fori_loop(0, LANES // 16, sixteen, 0, unroll=LANES // 16)


def steering_of(scale, mic_pos, grid_pos, masks, width):
    return pl.pallas_call(
        functools.partial(steering_kernel, masks=masks, width=width),
        out_shape=jax.ShapeDtypeStruct((len(masks), 2 * LANES, width), jnp.bfloat16),
        in_specs=[pl.BlockSpec(memory_space=pltpu.VMEM)] * 3,
        out_specs=pl.BlockSpec(memory_space=pltpu.VMEM),
        scratch_shapes=[pltpu.VMEM((LANES, 8), jnp.float32)],
        compiler_params=pltpu.CompilerParams(vmem_limit_bytes=32 * MIB),
        cost_estimate=pl.CostEstimate(
            flops=50 * len(masks) * LANES * width, bytes_accessed=4 * len(masks) * LANES * width, transcendentals=0
        ),
    )(scale, mic_pos, grid_pos)


def left_blocks(own, other, odd):
    pairs, rows, _ = own.shape
    own = own.astype(jnp.float32).reshape(pairs * rows, LANES)
    other = other.astype(jnp.float32).reshape(pairs * rows, LANES)
    lower = jnp.where(odd, other, own)
    upper = jnp.where(odd, own, other)
    half = lax.broadcasted_iota(jnp.int32, lower.shape, 1) < LANES // 2
    even_segs = jnp.where(half, lower, pltpu.roll(upper, LANES // 2, 1))
    odd_segs = jnp.where(half, pltpu.roll(lower, LANES // 2, 1), upper)
    return [x.reshape(pairs, rows, LANES) for x in (even_segs, odd_segs)]


def power_kernel(a_ref, b_ref, c_ref, d_ref, steer_ref, before_ref, out_ref, *, scale):
    odd = lax.bitwise_and(lax.axis_index("mic"), 1) == 1
    pieces = left_blocks(a_ref[...], b_ref[...], odd) + left_blocks(c_ref[...], d_ref[...], odd)
    pairs, rows, _ = a_ref.shape
    lines = rows // 2
    beams = None
    for k in range(pairs):
        left = []
        for piece in pieces:
            x = piece[k]
            turned = jnp.concatenate([-x[lines:], x[:lines]], axis=0)
            left.append(jnp.concatenate([x, turned], axis=1))
        left = jnp.concatenate(left, axis=0).astype(jnp.bfloat16)
        term = jnp.dot(left, steer_ref[k], preferred_element_type=jnp.float32)
        beams = term if beams is None else beams + term
    power = jnp.sum((beams * beams).reshape(-1, 8, beams.shape[1]), axis=0) + before_ref[...]
    if scale is None:
        out_ref[...] = power
    else:
        out_ref[...] = jnp.sum(power, axis=0, keepdims=True) / jnp.float32(scale)


def power_of(blocks, steering, before, scale):
    width = steering.shape[2]
    shape = (8 if scale is None else 1, width)
    pairs, rows, _ = blocks[0].shape
    return pl.pallas_call(
        functools.partial(power_kernel, scale=scale),
        out_shape=jax.ShapeDtypeStruct(shape, jnp.float32),
        in_specs=[pl.BlockSpec(memory_space=pltpu.VMEM)] * 6,
        out_specs=pl.BlockSpec(memory_space=pltpu.VMEM),
        compiler_params=pltpu.CompilerParams(vmem_limit_bytes=32 * MIB),
        cost_estimate=pl.CostEstimate(
            flops=2 * 4 * rows * steering.size, bytes_accessed=2 * steering.size, transcendentals=0
        ),
    )(*blocks, steering, before)


def shards(time_data, order_bin, mic_pos, grid_pos):
    seg_dev, mic_dev, samples = time_data.shape
    seg_count = lax.axis_size("seg")
    mic_count = lax.axis_size("mic")
    own_width = grid_pos.shape[1] // seg_count
    denom = seg_count * seg_dev * mic_count * mic_dev * 0.375 * samples

    def swap(x, mask):
        pairs = [(i, i ^ mask) for i in range(seg_count * mic_count)]
        return lax.ppermute(x, ("seg", "mic"), pairs)

    spectra, scale = spectra_of(order_bin, time_data)
    masks = [0]
    bit = mic_count // 2
    while bit > 1:
        masks += [m ^ (bit // 2) for m in masks]
        bit //= 2
    steering = steering_of(scale, mic_pos, grid_pos, masks, own_width)
    held = spectra[None]
    bit = mic_count // 2
    while bit > 1:
        came = swap(held, bit)
        if bit == mic_count // 2:
            came, steering = lax.optimization_barrier((came, steering))
        held = jnp.concatenate([held, came], axis=0)
        bit //= 2
    far = 2 * mic_count
    both = swap(held, far + 1)
    beside = swap(held, 1)
    across = swap(held, far)
    blocks = [held, beside, across, both]
    twin = swap(jnp.concatenate(blocks, axis=0), mic_count)
    pairs = len(masks)
    twins = [twin[i * pairs : (i + 1) * pairs] for i in range(4)]
    half = power_of(blocks, steering, jnp.zeros((8, own_width), jnp.float32), None)
    return power_of(twins, steering, half, denom)


def solution(mesh):
    placed = (P("seg", "mic", None), P(), P(), P(None, "mic"))
    return jax.shard_map(
        shards, mesh=mesh, in_specs=placed, out_specs=P("mic", "seg"), check_vma=False
    )
```

```python
import functools
import math

import jax
import jax.numpy as jnp
import numpy as np
from jax import lax
from jax.experimental import pallas as pl
from jax.experimental.pallas import tpu as pltpu
from jax.sharding import PartitionSpec as P

LANES = 128
MIB = 1024 * 1024
NEAREST = 1.5 * 2.0**23


def fitted(values, degree):
    count = degree + 1
    nodes = 0.125 + 0.125 * np.cos((2 * np.arange(count) + 1) * np.pi / (2 * count))
    return [float(c) for c in np.linalg.solve(np.vander(nodes, count, increasing=True), values(nodes))]


COS_FIT = fitted(lambda q: np.cos(2 * np.pi * np.sqrt(q)), 6)
SIN_FIT = fitted(lambda q: np.sin(2 * np.pi * np.sqrt(q)) / np.sqrt(q), 5)


def horner(coefficients, q):
    total = q * coefficients[-1] + coefficients[-2]
    for c in coefficients[-3::-1]:
        total = total * q + c
    return total


def cos_sin_turns(turns):
    r = turns - ((turns + NEAREST) - NEAREST)
    q = r * r
    return horner(COS_FIT, q), r * horner(SIN_FIT, q)


def in_hbm(x):
    return pltpu.with_memory_space_constraint(x, pltpu.HBM)


def window_kernel(out_ref):
    times = lax.broadcasted_iota(jnp.int32, out_ref.shape, 1)
    cos_w, _ = cos_sin_turns(times.astype(jnp.float32) * (1.0 / out_ref.shape[1]))
    out_ref[...] = 0.5 - 0.5 * cos_w


def window_of(samples):
    return pl.pallas_call(
        window_kernel,
        out_shape=jax.ShapeDtypeStruct((8, samples), jnp.float32),
        out_specs=pl.BlockSpec(memory_space=pltpu.VMEM),
        compiler_params=pltpu.CompilerParams(vmem_limit_bytes=16 * MIB),
        cost_estimate=pl.CostEstimate(flops=8 * 2**30, bytes_accessed=2**24, transcendentals=0),
    )()


def table_of(order, window):
    samples = window.shape[1]
    times = lax.broadcasted_iota(jnp.int32, window.shape, 1)
    row = lax.broadcasted_iota(jnp.int32, window.shape, 0)
    turned = lax.rem(order * times, jnp.int32(samples))
    cos_a, sin_a = cos_sin_turns(turned.astype(jnp.float32) * (1.0 / samples))
    table = jnp.where(row == 0, window * cos_a, jnp.where(row == 1, -(window * sin_a), 0.0))
    return table.astype(jnp.bfloat16)


def steer(order, samples, points, mic_ref, steer_ref, column, first_pair):
    per_mm = order.astype(jnp.float32) * jnp.float32(51200.0 / 343.0 / 1000.0 / samples)
    for k in range(steer_ref.shape[0]):
        pair = first_pair + k
        mics = mic_ref[:, pair * LANES : (pair + 1) * LANES].astype(jnp.float32)
        mics = jnp.concatenate([mics, jnp.zeros((5, LANES), jnp.float32)], axis=0)
        column[...] = jnp.transpose(mics)

        def sixteen(i, carry, k=k):
            first = pl.multiple_of(i * 16, 16)
            mine = column[pl.ds(first, 16), :]
            square = None
            for axis in range(3):
                gap = points[axis : axis + 1, :] - mine[:, axis : axis + 1]
                square = gap * gap if square is None else square + gap * gap
            turns = square * lax.rsqrt(jnp.maximum(square, 1.0)) * per_mm
            cosine, sine = cos_sin_turns(turns)
            steer_ref[k, pl.ds(first, 16), :] = cosine.astype(jnp.bfloat16)
            steer_ref[k, pl.ds(LANES + first, 16), :] = sine.astype(jnp.bfloat16)
            return carry

        lax.fori_loop(0, LANES // 16, sixteen, 0, unroll=LANES // 16)


def own_points(grid_ref, width):
    offset = pl.multiple_of(lax.axis_index(("row", "core")) * width, width)
    return grid_ref[:, pl.ds(offset, width)].astype(jnp.float32)


def setup_kernel(order_ref, window_ref, mic_ref, grid_ref, table_ref, steer_ref, column, *, width):
    table_ref[...] = table_of(order_ref[0], window_ref[...])
    samples = table_ref.shape[1]
    steer(order_ref[0], samples, own_points(grid_ref, width), mic_ref, steer_ref, column, 0)


def setup_of(order_bin, window, mic_pos, grid_pos, pairs, width):
    samples = window.shape[1]
    return pl.pallas_call(
        functools.partial(setup_kernel, width=width),
        out_shape=[
            jax.ShapeDtypeStruct((8, samples), jnp.bfloat16),
            jax.ShapeDtypeStruct((pairs, 2 * LANES, width), jnp.bfloat16),
        ],
        in_specs=[pl.BlockSpec(memory_space=pltpu.SMEM)] + [pl.BlockSpec(memory_space=pltpu.VMEM)] * 3,
        out_specs=[pl.BlockSpec(memory_space=pltpu.VMEM)] * 2,
        scratch_shapes=[pltpu.VMEM((LANES, 8), jnp.float32)],
        compiler_params=pltpu.CompilerParams(vmem_limit_bytes=16 * MIB),
        cost_estimate=pl.CostEstimate(flops=2 * 2**30, bytes_accessed=2**22, transcendentals=0),
    )(order_bin, window, mic_pos, grid_pos)


def spectra_kernel(table_ref, data_ref, out_ref, rows_ref):
    seg, mic, samples = data_ref.shape
    lines = seg * mic // LANES
    block = data_ref[...].reshape(seg * mic, samples)
    spec = lax.dot_general(
        table_ref[...], block, (((1,), (1,)), ((), ())), preferred_element_type=jnp.float32
    )
    for line in range(lines):
        rows_ref[pl.ds(line, 1), :] = spec[0:1, line * LANES : (line + 1) * LANES]
        rows_ref[pl.ds(lines + line, 1), :] = spec[1:2, line * LANES : (line + 1) * LANES]
    out_ref[...] = rows_ref[...].astype(jnp.bfloat16)


def spectra_of(table, time_data):
    seg, mic, samples = time_data.shape
    lines = seg * mic // LANES
    return pl.pallas_call(
        spectra_kernel,
        out_shape=jax.ShapeDtypeStruct((2 * lines, LANES), jnp.bfloat16),
        in_specs=[pl.BlockSpec(memory_space=pltpu.VMEM)] * 2,
        out_specs=pl.BlockSpec(memory_space=pltpu.VMEM),
        scratch_shapes=[pltpu.VMEM((2 * lines, LANES), jnp.float32)],
        compiler_params=pltpu.CompilerParams(vmem_limit_bytes=16 * MIB),
        cost_estimate=pl.CostEstimate(
            flops=4 * time_data.size, bytes_accessed=2 * time_data.size, transcendentals=0
        ),
    )(table, time_data)


def steering_kernel(order_ref, mic_ref, grid_ref, out_ref, column, *, first_pair, samples, width):
    steer(order_ref[0], samples, own_points(grid_ref, width), mic_ref, out_ref, column, first_pair)


def steering_of(order_bin, mic_pos, grid_pos, first_pair, samples, width):
    pairs = mic_pos.shape[1] // LANES - first_pair
    return pl.pallas_call(
        functools.partial(steering_kernel, first_pair=first_pair, samples=samples, width=width),
        out_shape=jax.ShapeDtypeStruct((pairs, 2 * LANES, width), jnp.bfloat16),
        in_specs=[pl.BlockSpec(memory_space=pltpu.SMEM)] + [pl.BlockSpec(memory_space=pltpu.VMEM)] * 2,
        out_specs=pl.BlockSpec(memory_space=pltpu.VMEM),
        scratch_shapes=[pltpu.VMEM((LANES, 8), jnp.float32)],
        compiler_params=pltpu.CompilerParams(vmem_limit_bytes=16 * MIB),
        cost_estimate=pl.CostEstimate(
            flops=50 * pairs * LANES * width, bytes_accessed=4 * pairs * LANES * width, transcendentals=0
        ),
    )(order_bin, mic_pos, grid_pos)


def power_kernel(spec_ref, steer_a_ref, steer_b_ref, before_ref, out_ref, *, scale):
    groups, pairs, _, rows, _ = spec_ref.shape
    lines = rows // 2
    half = lax.broadcasted_iota(jnp.int32, (rows, LANES), 1) < LANES // 2
    beams = None
    for k in range(pairs):
        left = []
        for g in range(groups):
            lower = spec_ref[g, k, 0].astype(jnp.float32)
            upper = spec_ref[g, k, 1].astype(jnp.float32)
            even_segs = jnp.where(half, lower, pltpu.roll(upper, LANES // 2, 1))
            odd_segs = jnp.where(half, pltpu.roll(lower, LANES // 2, 1), upper)
            for x in (even_segs, odd_segs):
                turned = jnp.concatenate([-x[lines:], x[:lines]], axis=0)
                left.append(jnp.concatenate([x, turned], axis=1))
        left = jnp.concatenate(left, axis=0).astype(jnp.bfloat16)
        cut = steer_a_ref.shape[0]
        steering = steer_a_ref[k] if k < cut else steer_b_ref[k - cut]
        term = jnp.dot(left, steering, preferred_element_type=jnp.float32)
        beams = term if beams is None else beams + term
    power = jnp.sum((beams * beams).reshape(-1, 8, beams.shape[1]), axis=0) + before_ref[...]
    if scale is None:
        out_ref[...] = power
    else:
        out_ref[...] = jnp.sum(power, axis=0, keepdims=True) / jnp.float32(scale)


def power_of(spectra, steering, before, scale):
    width = steering[0].shape[2]
    size = 2 * steering[0].size
    shape = (8 if scale is None else 1, width)
    return pl.pallas_call(
        functools.partial(power_kernel, scale=scale),
        out_shape=jax.ShapeDtypeStruct(shape, jnp.float32),
        in_specs=[pl.BlockSpec(memory_space=pltpu.VMEM)] * 4,
        out_specs=pl.BlockSpec(memory_space=pltpu.VMEM),
        compiler_params=pltpu.CompilerParams(vmem_limit_bytes=16 * MIB),
        cost_estimate=pl.CostEstimate(
            flops=2 * 128 * size, bytes_accessed=2 * size, transcendentals=0
        ),
    )(spectra, *steering, before)


def shards(time_data, order_bin, mic_pos, grid_pos):
    seg_dev, mic_dev, samples = time_data.shape
    rows = lax.axis_size("row")
    seg_count = rows * lax.axis_size("core")
    mic_count = lax.axis_size("mic")
    own_width = grid_pos.shape[1] // seg_count
    denom = seg_count * seg_dev * mic_count * mic_dev * 0.375 * samples
    early = 3 * (mic_count // 2) // 4
    window, order_bin = lax.optimization_barrier((window_of(samples), order_bin))
    table, steering_a = setup_of(order_bin, window, mic_pos, grid_pos, early, own_width)
    spectra = spectra_of(table, time_data)
    every = jnp.broadcast_to(spectra[None], (rows * mic_count,) + spectra.shape)
    every = lax.all_to_all(every, ("row", "mic"), 0, 0, tiled=True)
    twin = lax.ppermute(every, "core", [(0, 1), (1, 0)])
    every, later_order = lax.optimization_barrier((every, order_bin))
    steering = (steering_a, steering_of(later_order, mic_pos, grid_pos, early, samples, own_width))
    shape = (rows, mic_count // 2, 2) + spectra.shape
    half = power_of(every.reshape(shape), steering, jnp.zeros((8, own_width), jnp.float32), None)
    return power_of(twin.reshape(shape), steering, half, denom)


def solution(mesh):
    seg_count, mic_count = mesh.shape["seg"], mesh.shape["mic"]
    split = jax.sharding.Mesh(
        mesh.devices.reshape(seg_count // 2, 2, mic_count), ("row", "core", "mic")
    )
    seg = ("row", "core")
    placed = (P(seg, "mic", None), P(), P(), P(None, "mic"))
    return jax.shard_map(
        shards, mesh=split, in_specs=placed, out_specs=P("mic", seg), check_vma=False
    )
```

```python
import functools
import math

import jax
import jax.numpy as jnp
import numpy as np
from jax import lax
from jax.experimental import pallas as pl
from jax.experimental.pallas import tpu as pltpu
from jax.sharding import PartitionSpec as P

LANES = 128
MIB = 1024 * 1024
NEAREST = 1.5 * 2.0**23


def fitted(values, degree):
    count = degree + 1
    nodes = 0.125 + 0.125 * np.cos((2 * np.arange(count) + 1) * np.pi / (2 * count))
    return [float(c) for c in np.linalg.solve(np.vander(nodes, count, increasing=True), values(nodes))]


COS_FIT = fitted(lambda q: np.cos(2 * np.pi * np.sqrt(q)), 6)
SIN_FIT = fitted(lambda q: np.sin(2 * np.pi * np.sqrt(q)) / np.sqrt(q), 5)


def horner(coefficients, q):
    total = q * coefficients[-1] + coefficients[-2]
    for c in coefficients[-3::-1]:
        total = total * q + c
    return total


def cos_sin_turns(turns):
    r = turns - ((turns + NEAREST) - NEAREST)
    q = r * r
    return horner(COS_FIT, q), r * horner(SIN_FIT, q)


def in_hbm(x):
    return pltpu.with_memory_space_constraint(x, pltpu.HBM)


def window_kernel(out_ref):
    times = lax.broadcasted_iota(jnp.int32, out_ref.shape, 1)
    cos_w, _ = cos_sin_turns(times.astype(jnp.float32) * (1.0 / out_ref.shape[1]))
    out_ref[...] = 0.5 - 0.5 * cos_w


def window_of(samples):
    return pl.pallas_call(
        window_kernel,
        out_shape=jax.ShapeDtypeStruct((8, samples), jnp.float32),
        out_specs=pl.BlockSpec(memory_space=pltpu.VMEM),
        compiler_params=pltpu.CompilerParams(vmem_limit_bytes=16 * MIB),
        cost_estimate=pl.CostEstimate(flops=8 * 2**30, bytes_accessed=2**24, transcendentals=0),
    )()


def table_of(order, window):
    samples = window.shape[1]
    times = lax.broadcasted_iota(jnp.int32, window.shape, 1)
    row = lax.broadcasted_iota(jnp.int32, window.shape, 0)
    turned = lax.rem(order * times, jnp.int32(samples))
    cos_a, sin_a = cos_sin_turns(turned.astype(jnp.float32) * (1.0 / samples))
    table = jnp.where(row == 0, window * cos_a, jnp.where(row == 1, -(window * sin_a), 0.0))
    return table.astype(jnp.bfloat16)


def steer(order, samples, points, mic_ref, steer_ref, column, first_pair):
    per_mm = order.astype(jnp.float32) * jnp.float32(51200.0 / 343.0 / 1000.0 / samples)
    half = LANES // 2
    for k in range(steer_ref.shape[0]):
        pair = first_pair + k
        mics = mic_ref[:, pair * LANES : (pair + 1) * LANES].astype(jnp.float32)
        mics = jnp.concatenate([mics, jnp.zeros((5, LANES), jnp.float32)], axis=0)
        column[...] = jnp.transpose(mics)
        for first in range(0, LANES, 16):
            mine = column[first : first + 16, :]
            square = None
            for axis in range(3):
                gap = points[axis : axis + 1, :] - mine[:, axis : axis + 1]
                square = gap * gap if square is None else square + gap * gap
            turns = square * lax.rsqrt(jnp.maximum(square, 1.0)) * per_mm
            cosine, sine = cos_sin_turns(turns)
            row = first // half * LANES + first % half
            steer_ref[k, row : row + 16, :] = cosine.astype(jnp.bfloat16)
            steer_ref[k, row + half : row + half + 16, :] = (-sine).astype(jnp.bfloat16)


def own_points(grid_ref, width):
    offset = pl.multiple_of(lax.axis_index(("row", "core")) * width, width)
    return grid_ref[:, pl.ds(offset, width)].astype(jnp.float32)


def setup_kernel(order_ref, window_ref, mic_ref, grid_ref, table_ref, steer_ref, column, *, width):
    table_ref[...] = table_of(order_ref[0], window_ref[...])
    samples = table_ref.shape[1]
    steer(order_ref[0], samples, own_points(grid_ref, width), mic_ref, steer_ref, column, 0)


def setup_of(order_bin, window, mic_pos, grid_pos, pairs, width):
    samples = window.shape[1]
    return pl.pallas_call(
        functools.partial(setup_kernel, width=width),
        out_shape=[
            jax.ShapeDtypeStruct((8, samples), jnp.bfloat16),
            jax.ShapeDtypeStruct((pairs, 2 * LANES, width), jnp.bfloat16),
        ],
        in_specs=[pl.BlockSpec(memory_space=pltpu.SMEM)] + [pl.BlockSpec(memory_space=pltpu.VMEM)] * 3,
        out_specs=[pl.BlockSpec(memory_space=pltpu.VMEM)] * 2,
        scratch_shapes=[pltpu.VMEM((LANES, 8), jnp.float32)],
        compiler_params=pltpu.CompilerParams(vmem_limit_bytes=16 * MIB),
        cost_estimate=pl.CostEstimate(flops=2 * 2**30, bytes_accessed=2**22, transcendentals=0),
    )(order_bin, window, mic_pos, grid_pos)


def spectra_kernel(table_ref, data_ref, out_ref, rows_ref):
    samples = data_ref.shape[1]
    lines = data_ref.shape[0] // LANES
    shares = (4, 4)
    table = table_ref[...]
    wide = table.astype(jnp.float32)
    factors = [
        [jnp.broadcast_to(wide[part : part + 1, c : c + LANES], (16, LANES)) for c in range(0, samples, LANES)]
        for part in range(2)
    ]
    on_matrix = []
    on_vector = []
    for first in range(0, lines, sum(shares)):
        group = min(shares[0], lines - first)
        if group:
            block = data_ref[pl.ds(first * LANES, group * LANES)]
            spec = lax.dot_general(
                table, block, (((1,), (1,)), ((), ())), preferred_element_type=jnp.float32
            )
            on_matrix.append((first, group, spec))
        for line in range(first + group, min(first + sum(shares), lines)):
            sums = ([], [])
            for top in range(0, LANES, 16):
                rows = data_ref[pl.ds(line * LANES + top, 16)].astype(jnp.float32)
                for part in range(2):
                    total = None
                    for c, factor in enumerate(factors[part]):
                        term = rows[:, c * LANES : (c + 1) * LANES] * factor
                        total = term if total is None else total + term
                    sums[part].append(total)
            for part in range(2):
                turned = jnp.transpose(jnp.concatenate(sums[part], axis=0))
                on_vector.append((part * lines + line, jnp.sum(turned.reshape(-1, 8, LANES), axis=0)))
    for first, group, spec in on_matrix:
        for j in range(group):
            for part in range(2):
                rows_ref[pl.ds(part * lines + first + j, 1), :] = spec[
                    part : part + 1, j * LANES : (j + 1) * LANES
                ]
    for row, eight in on_vector:
        rows_ref[pl.ds(row, 1), :] = jnp.sum(eight, axis=0, keepdims=True)
    real, imag = rows_ref[:lines], rows_ref[lines:]
    half = lax.broadcasted_iota(jnp.int32, real.shape, 1) < LANES // 2
    out_ref[:lines] = jnp.where(half, real, pltpu.roll(imag, LANES // 2, 1)).astype(jnp.bfloat16)
    out_ref[lines:] = jnp.where(half, pltpu.roll(real, LANES // 2, 1), imag).astype(jnp.bfloat16)


def spectra_of(table, time_data):
    seg, mic, samples = time_data.shape
    lines = seg * mic // LANES
    return pl.pallas_call(
        spectra_kernel,
        out_shape=jax.ShapeDtypeStruct((2 * lines, LANES), jnp.bfloat16),
        in_specs=[pl.BlockSpec(memory_space=pltpu.VMEM)] * 2,
        out_specs=pl.BlockSpec(memory_space=pltpu.VMEM),
        scratch_shapes=[pltpu.VMEM((2 * lines, LANES), jnp.float32)],
        compiler_params=pltpu.CompilerParams(vmem_limit_bytes=16 * MIB),
        cost_estimate=pl.CostEstimate(
            flops=4 * time_data.size, bytes_accessed=2 * time_data.size, transcendentals=0
        ),
    )(table, time_data.reshape(seg * mic, samples))


def steering_kernel(order_ref, mic_ref, grid_ref, out_ref, column, *, first_pair, samples, width):
    steer(order_ref[0], samples, own_points(grid_ref, width), mic_ref, out_ref, column, first_pair)


def steering_of(order_bin, mic_pos, grid_pos, first_pair, samples, width):
    pairs = mic_pos.shape[1] // LANES - first_pair
    return pl.pallas_call(
        functools.partial(steering_kernel, first_pair=first_pair, samples=samples, width=width),
        out_shape=jax.ShapeDtypeStruct((pairs, 2 * LANES, width), jnp.bfloat16),
        in_specs=[pl.BlockSpec(memory_space=pltpu.SMEM)] + [pl.BlockSpec(memory_space=pltpu.VMEM)] * 2,
        out_specs=pl.BlockSpec(memory_space=pltpu.VMEM),
        scratch_shapes=[pltpu.VMEM((LANES, 8), jnp.float32)],
        compiler_params=pltpu.CompilerParams(vmem_limit_bytes=16 * MIB),
        cost_estimate=pl.CostEstimate(
            flops=50 * pairs * LANES * width, bytes_accessed=4 * pairs * LANES * width, transcendentals=0
        ),
    )(order_bin, mic_pos, grid_pos)


def power_kernel(spec_ref, steer_a_ref, steer_b_ref, before_ref, out_ref, *, scale):
    groups, devices, segs, _ = spec_ref.shape
    cut = steer_a_ref.shape[0]
    half = lax.broadcasted_iota(jnp.int32, (segs, LANES), 1) < LANES // 2
    beams = None
    for k in range(devices // 2):
        real, imag = [], []
        for g in range(groups):
            both = [spec_ref[g, 2 * k + i] for i in range(2)]
            real.append(jnp.concatenate(both, axis=1))
            swapped = [jnp.where(half, pltpu.roll(x, LANES // 2, 1), -pltpu.roll(x, LANES // 2, 1)) for x in both]
            imag.append(jnp.concatenate(swapped, axis=1))
        left = jnp.concatenate(real + imag, axis=0)
        steering = steer_a_ref[k] if k < cut else steer_b_ref[k - cut]
        term = jnp.dot(left, steering, preferred_element_type=jnp.float32)
        beams = term if beams is None else beams + term
    power = jnp.sum((beams * beams).reshape(-1, 8, beams.shape[1]), axis=0) + before_ref[...]
    if scale is None:
        out_ref[...] = power
    else:
        out_ref[...] = jnp.sum(power, axis=0, keepdims=True) / jnp.float32(scale)


def power_of(spectra, steering, before, scale):
    width = steering[0].shape[2]
    size = 2 * steering[0].size
    shape = (8 if scale is None else 1, width)
    return pl.pallas_call(
        functools.partial(power_kernel, scale=scale),
        out_shape=jax.ShapeDtypeStruct(shape, jnp.float32),
        in_specs=[pl.BlockSpec(memory_space=pltpu.VMEM)] * 4,
        out_specs=pl.BlockSpec(memory_space=pltpu.VMEM),
        compiler_params=pltpu.CompilerParams(vmem_limit_bytes=16 * MIB),
        cost_estimate=pl.CostEstimate(
            flops=2 * 128 * size, bytes_accessed=2 * size, transcendentals=0
        ),
    )(spectra, *steering, before)


def shards(time_data, order_bin, mic_pos, grid_pos):
    seg_dev, mic_dev, samples = time_data.shape
    rows = lax.axis_size("row")
    seg_count = rows * lax.axis_size("core")
    mic_count = lax.axis_size("mic")
    own_width = grid_pos.shape[1] // seg_count
    denom = seg_count * seg_dev * mic_count * mic_dev * 0.375 * samples
    early = 3 * (mic_count // 2) // 4
    window, order_bin = lax.optimization_barrier((window_of(samples), order_bin))
    table, steering_a = setup_of(order_bin, window, mic_pos, grid_pos, early, own_width)
    spectra = spectra_of(table, time_data)
    cores = lax.axis_size("core")
    halves = spectra.reshape(1, cores, 1, spectra.shape[0] // cores, LANES)
    every = jnp.broadcast_to(halves, (rows, cores, mic_count) + halves.shape[3:])
    every = every.reshape((seg_count * mic_count,) + halves.shape[3:])
    every = lax.all_to_all(every, ("row", "core", "mic"), 0, 0, tiled=True)
    twin = lax.ppermute(every, "core", [(0, 1), (1, 0)])
    every, later_order = lax.optimization_barrier((every, order_bin))
    steering = (steering_a, steering_of(later_order, mic_pos, grid_pos, early, samples, own_width))
    shape = (seg_count, mic_count) + halves.shape[3:]
    half = power_of(every.reshape(shape), steering, jnp.zeros((8, own_width), jnp.float32), None)
    return power_of(twin.reshape(shape), steering, half, denom)


def solution(mesh):
    seg_count, mic_count = mesh.shape["seg"], mesh.shape["mic"]
    split = jax.sharding.Mesh(
        mesh.devices.reshape(seg_count // 2, 2, mic_count), ("row", "core", "mic")
    )
    seg = ("row", "core")
    placed = (P(seg, "mic", None), P(), P(), P(None, "mic"))
    return jax.shard_map(
        shards, mesh=split, in_specs=placed, out_specs=P("mic", seg), check_vma=False
    )
```

```python
import functools

import jax
import jax.numpy as jnp
import numpy as np
from jax import lax
from jax.experimental import pallas as pl
from jax.experimental.pallas import tpu as pltpu
from jax.sharding import PartitionSpec as P

LANES = 128
MIB = 1024 * 1024
NEAREST = 1.5 * 2.0**23


def fitted(values, degree):
    count = degree + 1
    nodes = 0.125 + 0.125 * np.cos((2 * np.arange(count) + 1) * np.pi / (2 * count))
    return [float(c) for c in np.linalg.solve(np.vander(nodes, count, increasing=True), values(nodes))]


COS_FIT = fitted(lambda q: np.cos(2 * np.pi * np.sqrt(q)), 6)
SIN_FIT = fitted(lambda q: np.sin(2 * np.pi * np.sqrt(q)) / np.sqrt(q), 5)


def horner(coefficients, q):
    total = q * coefficients[-1] + coefficients[-2]
    for c in coefficients[-3::-1]:
        total = total * q + c
    return total


def cos_sin_turns(turns):
    r = turns - ((turns + NEAREST) - NEAREST)
    q = r * r
    return horner(COS_FIT, q), r * horner(SIN_FIT, q)


def window_kernel(out_ref):
    times = lax.broadcasted_iota(jnp.int32, out_ref.shape, 1)
    cos_w, _ = cos_sin_turns(times.astype(jnp.float32) * (1.0 / out_ref.shape[1]))
    out_ref[...] = 0.5 - 0.5 * cos_w


def window_of(samples):
    return pl.pallas_call(
        window_kernel,
        out_shape=jax.ShapeDtypeStruct((8, samples), jnp.float32),
        out_specs=pl.BlockSpec(memory_space=pltpu.VMEM),
        compiler_params=pltpu.CompilerParams(vmem_limit_bytes=16 * MIB),
        cost_estimate=pl.CostEstimate(flops=8 * 2**30, bytes_accessed=2**24, transcendentals=0),
    )()


def table_of(order, window):
    samples = window.shape[1]
    times = lax.broadcasted_iota(jnp.int32, window.shape, 1)
    row = lax.broadcasted_iota(jnp.int32, window.shape, 0)
    turned = lax.rem(order * times, jnp.int32(samples))
    cos_a, sin_a = cos_sin_turns(turned.astype(jnp.float32) * (1.0 / samples))
    table = jnp.where(row == 0, window * cos_a, jnp.where(row == 1, -(window * sin_a), 0.0))
    return table.astype(jnp.bfloat16)


def steer(order, samples, points, mic_ref, steer_ref, column, first_pair):
    per_mm = order.astype(jnp.float32) * jnp.float32(51200.0 / 343.0 / 1000.0 / samples)
    half = LANES // 2
    for k in range(steer_ref.shape[0]):
        pair = first_pair + k
        mics = mic_ref[:, pair * LANES : (pair + 1) * LANES].astype(jnp.float32)
        mics = jnp.concatenate([mics, jnp.zeros((5, LANES), jnp.float32)], axis=0)
        column[...] = jnp.transpose(mics)
        for first in range(0, LANES, 16):
            mine = column[first : first + 16, :]
            square = None
            for axis in range(3):
                gap = points[axis : axis + 1, :] - mine[:, axis : axis + 1]
                square = gap * gap if square is None else square + gap * gap
            turns = square * lax.rsqrt(jnp.maximum(square, 1.0)) * per_mm
            cosine, sine = cos_sin_turns(turns)
            row = first // half * LANES + first % half
            steer_ref[k, row : row + 16, :] = cosine.astype(jnp.bfloat16)
            steer_ref[k, row + half : row + half + 16, :] = (-sine).astype(jnp.bfloat16)


def own_points(grid_ref, width):
    offset = pl.multiple_of(lax.axis_index(("row", "core")) * width, width)
    return grid_ref[:, pl.ds(offset, width)].astype(jnp.float32)


def setup_kernel(order_ref, window_ref, mic_ref, grid_ref, table_ref, steer_ref, column, *, width):
    table_ref[...] = table_of(order_ref[0], window_ref[...])
    samples = table_ref.shape[1]
    steer(order_ref[0], samples, own_points(grid_ref, width), mic_ref, steer_ref, column, 0)


def setup_of(order_bin, window, mic_pos, grid_pos, pairs, width):
    samples = window.shape[1]
    return pl.pallas_call(
        functools.partial(setup_kernel, width=width),
        out_shape=[
            jax.ShapeDtypeStruct((8, samples), jnp.bfloat16),
            jax.ShapeDtypeStruct((pairs, 2 * LANES, width), jnp.bfloat16),
        ],
        in_specs=[pl.BlockSpec(memory_space=pltpu.SMEM)] + [pl.BlockSpec(memory_space=pltpu.VMEM)] * 3,
        out_specs=[pl.BlockSpec(memory_space=pltpu.VMEM)] * 2,
        scratch_shapes=[pltpu.VMEM((LANES, 8), jnp.float32)],
        compiler_params=pltpu.CompilerParams(vmem_limit_bytes=16 * MIB),
        cost_estimate=pl.CostEstimate(flops=2 * 2**30, bytes_accessed=2**22, transcendentals=0),
    )(order_bin, window, mic_pos, grid_pos)


def spectra_kernel(table_ref, data_ref, out_ref, rows_ref):
    samples = data_ref.shape[1]
    lines = data_ref.shape[0] // LANES
    on_each = 4
    table = table_ref[...]
    wide = table.astype(jnp.float32)
    factors = [
        [jnp.broadcast_to(wide[part : part + 1, c : c + LANES], (16, LANES)) for c in range(0, samples, LANES)]
        for part in range(2)
    ]
    on_matrix = []
    on_vector = []
    for first in range(0, lines, 2 * on_each):
        block = data_ref[pl.ds(first * LANES, on_each * LANES)]
        spec = lax.dot_general(
            table, block, (((1,), (1,)), ((), ())), preferred_element_type=jnp.float32
        )
        on_matrix.append((first, spec))
        for line in range(first + on_each, first + 2 * on_each):
            sums = ([], [])
            for top in range(0, LANES, 16):
                rows = data_ref[pl.ds(line * LANES + top, 16)].astype(jnp.float32)
                for part in range(2):
                    total = None
                    for c, factor in enumerate(factors[part]):
                        term = rows[:, c * LANES : (c + 1) * LANES] * factor
                        total = term if total is None else total + term
                    sums[part].append(total)
            for part in range(2):
                turned = jnp.transpose(jnp.concatenate(sums[part], axis=0))
                on_vector.append((part * lines + line, jnp.sum(turned.reshape(-1, 8, LANES), axis=0)))
    for first, spec in on_matrix:
        for j in range(on_each):
            for part in range(2):
                rows_ref[pl.ds(part * lines + first + j, 1), :] = spec[
                    part : part + 1, j * LANES : (j + 1) * LANES
                ]
    for row, eight in on_vector:
        rows_ref[pl.ds(row, 1), :] = jnp.sum(eight, axis=0, keepdims=True)
    real, imag = rows_ref[:lines], rows_ref[lines:]
    half = lax.broadcasted_iota(jnp.int32, real.shape, 1) < LANES // 2
    even = jnp.where(half, real, pltpu.roll(imag, LANES // 2, 1)).astype(jnp.bfloat16)
    odd = jnp.where(half, pltpu.roll(real, LANES // 2, 1), imag).astype(jnp.bfloat16)
    rows, _, mics = out_ref.shape[:3]
    for row in range(rows):
        for mic in range(mics):
            out_ref[row, 0, mic] = even
            out_ref[row, 1, mic] = odd


def spectra_of(table, time_data, devices):
    seg, mic, samples = time_data.shape
    lines = seg * mic // LANES
    return pl.pallas_call(
        spectra_kernel,
        out_shape=jax.ShapeDtypeStruct(devices + (lines, LANES), jnp.bfloat16),
        in_specs=[pl.BlockSpec(memory_space=pltpu.VMEM)] * 2,
        out_specs=pl.BlockSpec(memory_space=pltpu.VMEM),
        scratch_shapes=[pltpu.VMEM((2 * lines, LANES), jnp.float32)],
        compiler_params=pltpu.CompilerParams(vmem_limit_bytes=16 * MIB),
        cost_estimate=pl.CostEstimate(
            flops=4 * time_data.size, bytes_accessed=2 * time_data.size, transcendentals=0
        ),
    )(table, time_data.reshape(seg * mic, samples))


def steering_kernel(order_ref, mic_ref, grid_ref, out_ref, column, *, first_pair, samples, width):
    steer(order_ref[0], samples, own_points(grid_ref, width), mic_ref, out_ref, column, first_pair)


def steering_of(order_bin, mic_pos, grid_pos, first_pair, samples, width):
    pairs = mic_pos.shape[1] // LANES - first_pair
    return pl.pallas_call(
        functools.partial(steering_kernel, first_pair=first_pair, samples=samples, width=width),
        out_shape=jax.ShapeDtypeStruct((pairs, 2 * LANES, width), jnp.bfloat16),
        in_specs=[pl.BlockSpec(memory_space=pltpu.SMEM)] + [pl.BlockSpec(memory_space=pltpu.VMEM)] * 2,
        out_specs=pl.BlockSpec(memory_space=pltpu.VMEM),
        scratch_shapes=[pltpu.VMEM((LANES, 8), jnp.float32)],
        compiler_params=pltpu.CompilerParams(vmem_limit_bytes=16 * MIB),
        cost_estimate=pl.CostEstimate(
            flops=50 * pairs * LANES * width, bytes_accessed=4 * pairs * LANES * width, transcendentals=0
        ),
    )(order_bin, mic_pos, grid_pos)


def power_kernel(spec_ref, steer_a_ref, steer_b_ref, before_ref, out_ref, *, scale):
    groups, devices, segs, _ = spec_ref.shape
    width = out_ref.shape[1]
    half = lax.broadcasted_iota(jnp.int32, (segs, LANES), 1) < LANES // 2
    real, imag = [], []
    for g in range(groups):
        blocks = [spec_ref[g, d] for d in range(devices)]
        real.append(jnp.concatenate(blocks, axis=1))
        turned = [pltpu.roll(x, LANES // 2, 1) for x in blocks]
        imag.append(jnp.concatenate([jnp.where(half, x, -x) for x in turned], axis=1))
    left = jnp.concatenate(real + imag, axis=0)
    beams = None
    start = 0
    for ref in (steer_a_ref, steer_b_ref):
        depth = ref.shape[0] * ref.shape[1]
        term = jnp.dot(
            left[:, start : start + depth], ref[...].reshape(depth, width), preferred_element_type=jnp.float32
        )
        beams = term if beams is None else beams + term
        start += depth
    power = jnp.sum((beams * beams).reshape(-1, 8, width), axis=0) + before_ref[...]
    if scale is None:
        out_ref[...] = power
    else:
        out_ref[...] = jnp.sum(power, axis=0, keepdims=True) / jnp.float32(scale)


def power_of(spectra, steering, before, scale):
    width = steering[0].shape[2]
    size = 2 * steering[0].size
    shape = (8 if scale is None else 1, width)
    return pl.pallas_call(
        functools.partial(power_kernel, scale=scale),
        out_shape=jax.ShapeDtypeStruct(shape, jnp.float32),
        in_specs=[pl.BlockSpec(memory_space=pltpu.VMEM)] * 4,
        out_specs=pl.BlockSpec(memory_space=pltpu.VMEM),
        compiler_params=pltpu.CompilerParams(vmem_limit_bytes=16 * MIB),
        cost_estimate=pl.CostEstimate(
            flops=2 * 128 * size, bytes_accessed=2 * size, transcendentals=0
        ),
    )(spectra, *steering, before)


def shards(time_data, order_bin, mic_pos, grid_pos):
    seg_dev, mic_dev, samples = time_data.shape
    rows = lax.axis_size("row")
    cores = lax.axis_size("core")
    seg_count = rows * cores
    mic_count = lax.axis_size("mic")
    own_width = grid_pos.shape[1] // seg_count
    denom = seg_count * seg_dev * mic_count * mic_dev * 0.375 * samples
    early = 3 * (mic_count // 2) // 4
    window, order_bin = lax.optimization_barrier((window_of(samples), order_bin))
    table, steering_a = setup_of(order_bin, window, mic_pos, grid_pos, early, own_width)
    every = spectra_of(table, time_data, (rows, cores, mic_count))
    every = every.reshape((seg_count * mic_count,) + every.shape[3:])
    every = lax.all_to_all(every, ("row", "core", "mic"), 0, 0, tiled=True)
    twin = lax.ppermute(every, "core", [(0, 1), (1, 0)])
    every, later_order = lax.optimization_barrier((every, order_bin))
    steering = (steering_a, steering_of(later_order, mic_pos, grid_pos, early, samples, own_width))
    shape = (seg_count, mic_count) + every.shape[1:]
    half = power_of(every.reshape(shape), steering, jnp.zeros((8, own_width), jnp.float32), None)
    return power_of(twin.reshape(shape), steering, half, denom)


def solution(mesh):
    seg_count, mic_count = mesh.shape["seg"], mesh.shape["mic"]
    split = jax.sharding.Mesh(
        mesh.devices.reshape(seg_count // 2, 2, mic_count), ("row", "core", "mic")
    )
    seg = ("row", "core")
    placed = (P(seg, "mic", None), P(), P(), P(None, "mic"))
    return jax.shard_map(
        shards, mesh=split, in_specs=placed, out_specs=P("mic", seg), check_vma=False
    )
```

```python
import functools

import jax
import jax.numpy as jnp
import numpy as np
from jax import lax
from jax.experimental import pallas as pl
from jax.experimental.pallas import tpu as pltpu
from jax.sharding import PartitionSpec as P

LANES = 128
MIB = 1024 * 1024
NEAREST = 1.5 * 2.0**23


def fitted(values, degree):
    count = degree + 1
    nodes = 0.125 + 0.125 * np.cos((2 * np.arange(count) + 1) * np.pi / (2 * count))
    return [float(c) for c in np.linalg.solve(np.vander(nodes, count, increasing=True), values(nodes))]


COS_FIT = fitted(lambda q: np.cos(2 * np.pi * np.sqrt(q)), 6)
SIN_FIT = fitted(lambda q: np.sin(2 * np.pi * np.sqrt(q)) / np.sqrt(q), 5)


def horner(coefficients, q):
    total = q * coefficients[-1] + coefficients[-2]
    for c in coefficients[-3::-1]:
        total = total * q + c
    return total


def cos_sin_turns(turns):
    r = turns - ((turns + NEAREST) - NEAREST)
    q = r * r
    return horner(COS_FIT, q), r * horner(SIN_FIT, q)


def window_kernel(out_ref):
    times = lax.broadcasted_iota(jnp.int32, out_ref.shape, 1)
    cos_w, _ = cos_sin_turns(times.astype(jnp.float32) * (1.0 / out_ref.shape[1]))
    out_ref[...] = 0.5 - 0.5 * cos_w


def window_of(samples):
    return pl.pallas_call(
        window_kernel,
        out_shape=jax.ShapeDtypeStruct((8, samples), jnp.float32),
        out_specs=pl.BlockSpec(memory_space=pltpu.VMEM),
        compiler_params=pltpu.CompilerParams(vmem_limit_bytes=16 * MIB),
        cost_estimate=pl.CostEstimate(flops=8 * 2**30, bytes_accessed=2**24, transcendentals=0),
    )()


def table_of(order, window):
    samples = window.shape[1]
    times = lax.broadcasted_iota(jnp.int32, window.shape, 1)
    row = lax.broadcasted_iota(jnp.int32, window.shape, 0)
    turned = lax.rem(order * times, jnp.int32(samples))
    cos_a, sin_a = cos_sin_turns(turned.astype(jnp.float32) * (1.0 / samples))
    table = jnp.where(row == 0, window * cos_a, jnp.where(row == 1, -(window * sin_a), 0.0))
    return table.astype(jnp.bfloat16)


def steer(order, samples, points, mic_ref, steer_ref, column, first_pair):
    per_mm = order.astype(jnp.float32) * jnp.float32(51200.0 / 343.0 / 1000.0 / samples)
    half = LANES // 2
    for k in range(steer_ref.shape[0]):
        pair = first_pair + k
        mics = mic_ref[:, pair * LANES : (pair + 1) * LANES].astype(jnp.float32)
        mics = jnp.concatenate([mics, jnp.zeros((5, LANES), jnp.float32)], axis=0)
        column[...] = jnp.transpose(mics)
        for first in range(0, LANES, 16):
            mine = column[first : first + 16, :]
            square = None
            for axis in range(3):
                gap = points[axis : axis + 1, :] - mine[:, axis : axis + 1]
                square = gap * gap if square is None else square + gap * gap
            turns = square * lax.rsqrt(jnp.maximum(square, 1.0)) * per_mm
            cosine, sine = cos_sin_turns(turns)
            row = first // half * LANES + first % half
            steer_ref[k, row : row + 16, :] = cosine.astype(jnp.bfloat16)
            steer_ref[k, row + half : row + half + 16, :] = (-sine).astype(jnp.bfloat16)


def own_points(grid_ref, width):
    offset = pl.multiple_of(lax.axis_index(("row", "core")) * width, width)
    return grid_ref[:, pl.ds(offset, width)].astype(jnp.float32)


def setup_kernel(order_ref, window_ref, mic_ref, grid_ref, table_ref, steer_ref, column, *, width):
    table_ref[...] = table_of(order_ref[0], window_ref[...])
    samples = table_ref.shape[1]
    steer(order_ref[0], samples, own_points(grid_ref, width), mic_ref, steer_ref, column, 0)


def setup_of(order_bin, window, mic_pos, grid_pos, pairs, width):
    samples = window.shape[1]
    return pl.pallas_call(
        functools.partial(setup_kernel, width=width),
        out_shape=[
            jax.ShapeDtypeStruct((8, samples), jnp.bfloat16),
            jax.ShapeDtypeStruct((pairs, 2 * LANES, width), jnp.bfloat16),
        ],
        in_specs=[pl.BlockSpec(memory_space=pltpu.SMEM)] + [pl.BlockSpec(memory_space=pltpu.VMEM)] * 3,
        out_specs=[pl.BlockSpec(memory_space=pltpu.VMEM)] * 2,
        scratch_shapes=[pltpu.VMEM((LANES, 8), jnp.float32)],
        compiler_params=pltpu.CompilerParams(vmem_limit_bytes=16 * MIB),
        cost_estimate=pl.CostEstimate(flops=2 * 2**30, bytes_accessed=2**22, transcendentals=0),
    )(order_bin, window, mic_pos, grid_pos)


def spectra_kernel(table_ref, data_ref, out_ref):
    samples = data_ref.shape[1]
    lines = data_ref.shape[0] // LANES
    shares = (4, 4)
    table = table_ref[...]
    wide = table.astype(jnp.float32)
    factors = [
        [jnp.broadcast_to(wide[part : part + 1, c : c + LANES], (LANES, LANES)) for c in range(0, samples, LANES)]
        for part in range(2)
    ]
    pieces = ([], [])
    for first in range(0, lines, sum(shares)):
        block = data_ref[pl.ds(first * LANES, shares[0] * LANES)]
        spec = lax.dot_general(
            table, block, (((1,), (1,)), ((), ())), preferred_element_type=jnp.float32
        )
        for part in range(2):
            pieces[part].extend(spec[part : part + 1, j * LANES : (j + 1) * LANES] for j in range(shares[0]))
        for line in range(first + shares[0], first + sum(shares)):
            sums = [None, None]
            for c in range(samples // LANES):
                rows = data_ref[pl.ds(line * LANES, LANES), pl.ds(c * LANES, LANES)].astype(jnp.float32)
                for part in range(2):
                    term = rows * factors[part][c]
                    sums[part] = term if sums[part] is None else sums[part] + term
            for part in range(2):
                turned = jnp.transpose(sums[part])
                pieces[part].append(jnp.sum(turned, axis=0, keepdims=True))
    real, imag = (jnp.concatenate(x, axis=0) for x in pieces)
    half = lax.broadcasted_iota(jnp.int32, real.shape, 1) < LANES // 2
    even = jnp.where(half, real, pltpu.roll(imag, LANES // 2, 1)).astype(jnp.bfloat16)
    odd = jnp.where(half, pltpu.roll(real, LANES // 2, 1), imag).astype(jnp.bfloat16)
    rows, _, mics = out_ref.shape[:3]
    for row in range(rows):
        for mic in range(mics):
            out_ref[row, 0, mic] = even
            out_ref[row, 1, mic] = odd


def spectra_of(table, time_data, devices):
    seg, mic, samples = time_data.shape
    lines = seg * mic // LANES
    return pl.pallas_call(
        spectra_kernel,
        out_shape=jax.ShapeDtypeStruct(devices + (lines, LANES), jnp.bfloat16),
        in_specs=[pl.BlockSpec(memory_space=pltpu.VMEM)] * 2,
        out_specs=pl.BlockSpec(memory_space=pltpu.VMEM),
        compiler_params=pltpu.CompilerParams(vmem_limit_bytes=16 * MIB),
        cost_estimate=pl.CostEstimate(
            flops=4 * time_data.size, bytes_accessed=2 * time_data.size, transcendentals=0
        ),
    )(table, time_data.reshape(seg * mic, samples))


def steering_kernel(order_ref, mic_ref, grid_ref, out_ref, column, *, first_pair, samples, width):
    steer(order_ref[0], samples, own_points(grid_ref, width), mic_ref, out_ref, column, first_pair)


def steering_of(order_bin, mic_pos, grid_pos, first_pair, samples, width):
    pairs = mic_pos.shape[1] // LANES - first_pair
    return pl.pallas_call(
        functools.partial(steering_kernel, first_pair=first_pair, samples=samples, width=width),
        out_shape=jax.ShapeDtypeStruct((pairs, 2 * LANES, width), jnp.bfloat16),
        in_specs=[pl.BlockSpec(memory_space=pltpu.SMEM)] + [pl.BlockSpec(memory_space=pltpu.VMEM)] * 2,
        out_specs=pl.BlockSpec(memory_space=pltpu.VMEM),
        scratch_shapes=[pltpu.VMEM((LANES, 8), jnp.float32)],
        compiler_params=pltpu.CompilerParams(vmem_limit_bytes=16 * MIB),
        cost_estimate=pl.CostEstimate(
            flops=50 * pairs * LANES * width, bytes_accessed=4 * pairs * LANES * width, transcendentals=0
        ),
    )(order_bin, mic_pos, grid_pos)


def power_kernel(spec_ref, steer_a_ref, steer_b_ref, before_ref, out_ref, *, scale):
    groups, devices, segs, _ = spec_ref.shape
    width = out_ref.shape[1]
    half = lax.broadcasted_iota(jnp.int32, (segs, LANES), 1) < LANES // 2
    real, imag = [], []
    for g in range(groups):
        blocks = [spec_ref[g, d] for d in range(devices)]
        real.append(jnp.concatenate(blocks, axis=1))
        turned = [pltpu.roll(x, LANES // 2, 1) for x in blocks]
        imag.append(jnp.concatenate([jnp.where(half, x, -x) for x in turned], axis=1))
    left = jnp.concatenate(real + imag, axis=0)
    beams = None
    start = 0
    for ref in (steer_a_ref, steer_b_ref):
        depth = ref.shape[0] * ref.shape[1]
        term = jnp.dot(
            left[:, start : start + depth], ref[...].reshape(depth, width), preferred_element_type=jnp.float32
        )
        beams = term if beams is None else beams + term
        start += depth
    power = jnp.sum((beams * beams).reshape(-1, 8, width), axis=0) + before_ref[...]
    if scale is None:
        out_ref[...] = power
    else:
        out_ref[...] = jnp.sum(power, axis=0, keepdims=True) / jnp.float32(scale)


def power_of(spectra, steering, before, scale):
    width = steering[0].shape[2]
    size = 2 * steering[0].size
    shape = (8 if scale is None else 1, width)
    return pl.pallas_call(
        functools.partial(power_kernel, scale=scale),
        out_shape=jax.ShapeDtypeStruct(shape, jnp.float32),
        in_specs=[pl.BlockSpec(memory_space=pltpu.VMEM)] * 4,
        out_specs=pl.BlockSpec(memory_space=pltpu.VMEM),
        compiler_params=pltpu.CompilerParams(vmem_limit_bytes=16 * MIB),
        cost_estimate=pl.CostEstimate(
            flops=2 * 128 * size, bytes_accessed=2 * size, transcendentals=0
        ),
    )(spectra, *steering, before)


def shards(time_data, order_bin, mic_pos, grid_pos):
    seg_dev, mic_dev, samples = time_data.shape
    rows = lax.axis_size("row")
    cores = lax.axis_size("core")
    seg_count = rows * cores
    mic_count = lax.axis_size("mic")
    own_width = grid_pos.shape[1] // seg_count
    denom = seg_count * seg_dev * mic_count * mic_dev * 0.375 * samples
    early = 3 * (mic_count // 2) // 4
    window, order_bin = lax.optimization_barrier((window_of(samples), order_bin))
    table, steering_a = setup_of(order_bin, window, mic_pos, grid_pos, early, own_width)
    every = spectra_of(table, time_data, (rows, cores, mic_count))
    every = every.reshape((seg_count * mic_count,) + every.shape[3:])
    every = lax.all_to_all(every, ("row", "core", "mic"), 0, 0, tiled=True)
    twin = lax.ppermute(every, "core", [(0, 1), (1, 0)])
    every, later_order = lax.optimization_barrier((every, order_bin))
    steering = (steering_a, steering_of(later_order, mic_pos, grid_pos, early, samples, own_width))
    shape = (seg_count, mic_count) + every.shape[1:]
    half = power_of(every.reshape(shape), steering, jnp.zeros((8, own_width), jnp.float32), None)
    return power_of(twin.reshape(shape), steering, half, denom)


def solution(mesh):
    seg_count, mic_count = mesh.shape["seg"], mesh.shape["mic"]
    split = jax.sharding.Mesh(
        mesh.devices.reshape(seg_count // 2, 2, mic_count), ("row", "core", "mic")
    )
    seg = ("row", "core")
    placed = (P(seg, "mic", None), P(), P(), P(None, "mic"))
    return jax.shard_map(
        shards, mesh=split, in_specs=placed, out_specs=P("mic", seg), check_vma=False
    )
```

```python
import functools

import jax
import jax.numpy as jnp
import numpy as np
from jax import lax
from jax.experimental import pallas as pl
from jax.experimental.pallas import tpu as pltpu
from jax.sharding import PartitionSpec as P

LANES = 128
MIB = 1024 * 1024


def fitted(values, degree):
    count = degree + 1
    nodes = 0.125 + 0.125 * np.cos((2 * np.arange(count) + 1) * np.pi / (2 * count))
    return [float(c) for c in np.linalg.solve(np.vander(nodes, count, increasing=True), values(nodes))]


COS_FIT = fitted(lambda q: np.cos(2 * np.pi * np.sqrt(q)), 5)
MINUS_SIN_FIT = fitted(lambda q: -np.sin(2 * np.pi * np.sqrt(q)) / np.sqrt(q), 5)


def horner(coefficients, q):
    total = q * coefficients[-1] + coefficients[-2]
    for c in coefficients[-3::-1]:
        total = total * q + c
    return total


def cos_minus_sin(turns):
    r = turns - jnp.round(turns)
    q = r * r
    return horner(COS_FIT, q), r * horner(MINUS_SIN_FIT, q)


def lead_kernel(out_ref):
    out_ref[...] = jnp.zeros(out_ref.shape, out_ref.dtype)


def lead():
    return pl.pallas_call(
        lead_kernel,
        out_shape=jax.ShapeDtypeStruct((8, LANES), jnp.float32),
        out_specs=pl.BlockSpec(memory_space=pltpu.VMEM),
        compiler_params=pltpu.CompilerParams(vmem_limit_bytes=16 * MIB),
        cost_estimate=pl.CostEstimate(flops=8 * 2**30, bytes_accessed=2**24, transcendentals=0),
    )()


def table_of(order, samples):
    times = lax.broadcasted_iota(jnp.int32, (8, samples), 1)
    row = lax.broadcasted_iota(jnp.int32, (8, samples), 0)
    turned = lax.rem(order * times, jnp.int32(samples))
    cos_w, _ = cos_minus_sin(times.astype(jnp.float32) * (1.0 / samples))
    cos_a, minus_sin_a = cos_minus_sin(turned.astype(jnp.float32) * (1.0 / samples))
    window = 0.5 - 0.5 * cos_w
    table = jnp.where(row == 0, window * cos_a, jnp.where(row == 1, window * minus_sin_a, 0.0))
    return table.astype(jnp.bfloat16)


def steer(order, samples, points, mic_ref, steer_ref, column):
    per_mm = order.astype(jnp.float32) * jnp.float32(51200.0 / 343.0 / 1000.0 / samples)
    points = points * per_mm
    half = LANES // 2
    for k in range(steer_ref.shape[0]):
        mics = mic_ref[:, k * LANES : (k + 1) * LANES].astype(jnp.float32) * per_mm
        mics = jnp.concatenate([mics, jnp.zeros((5, LANES), jnp.float32)], axis=0)
        column[...] = jnp.transpose(mics)
        for first in range(0, LANES, 16):
            mine = column[first : first + 16, :]
            square = None
            for axis in range(3):
                gap = points[axis : axis + 1, :] - mine[:, axis : axis + 1]
                square = gap * gap if square is None else square + gap * gap
            turns = square * lax.rsqrt(jnp.maximum(square, 1e-12))
            cosine, minus_sine = cos_minus_sin(turns)
            row = first // half * LANES + first % half
            steer_ref[k, row : row + 16, :] = cosine.astype(jnp.bfloat16)
            steer_ref[k, row + half : row + half + 16, :] = minus_sine.astype(jnp.bfloat16)


def own_points(grid_ref, width):
    offset = pl.multiple_of(lax.axis_index(("row", "core")) * width, width)
    return grid_ref[:, pl.ds(offset, width)].astype(jnp.float32)


def setup_kernel(order_ref, lead_ref, mic_ref, grid_ref, table_ref, steer_ref, column, *, width):
    del lead_ref
    samples = table_ref.shape[1]
    table_ref[...] = table_of(order_ref[0], samples)
    steer(order_ref[0], samples, own_points(grid_ref, width), mic_ref, steer_ref, column)


def setup_of(order_bin, first, mic_pos, grid_pos, pairs, width, samples):
    return pl.pallas_call(
        functools.partial(setup_kernel, width=width),
        out_shape=[
            jax.ShapeDtypeStruct((8, samples), jnp.bfloat16),
            jax.ShapeDtypeStruct((pairs, 2 * LANES, width), jnp.bfloat16),
        ],
        in_specs=[pl.BlockSpec(memory_space=pltpu.SMEM)] + [pl.BlockSpec(memory_space=pltpu.VMEM)] * 3,
        out_specs=[pl.BlockSpec(memory_space=pltpu.VMEM)] * 2,
        scratch_shapes=[pltpu.VMEM((LANES, 8), jnp.float32)],
        compiler_params=pltpu.CompilerParams(vmem_limit_bytes=16 * MIB),
        cost_estimate=pl.CostEstimate(flops=2 * 2**30, bytes_accessed=2**22, transcendentals=0),
    )(order_bin, first, mic_pos, grid_pos)


def spectra_kernel(table_ref, data_ref, out_ref):
    samples = data_ref.shape[1]
    lines = data_ref.shape[0] // LANES
    shares = (4, 4)
    table = table_ref[...]
    wide = table.astype(jnp.float32)
    factors = [
        [jnp.broadcast_to(wide[part : part + 1, c : c + LANES], (LANES, LANES)) for c in range(0, samples, LANES)]
        for part in range(2)
    ]
    pieces = ([], [])
    for first in range(0, lines, sum(shares)):
        block = data_ref[pl.ds(first * LANES, shares[0] * LANES)]
        spec = lax.dot_general(
            table, block, (((1,), (1,)), ((), ())), preferred_element_type=jnp.float32
        )
        for part in range(2):
            pieces[part].extend(spec[part : part + 1, j * LANES : (j + 1) * LANES] for j in range(shares[0]))
        for line in range(first + shares[0], first + sum(shares)):
            sums = [None, None]
            for c in range(samples // LANES):
                rows = data_ref[pl.ds(line * LANES, LANES), pl.ds(c * LANES, LANES)].astype(jnp.float32)
                for part in range(2):
                    term = rows * factors[part][c]
                    sums[part] = term if sums[part] is None else sums[part] + term
            for part in range(2):
                turned = jnp.transpose(sums[part])
                pieces[part].append(jnp.sum(turned, axis=0, keepdims=True))
    real, imag = (jnp.concatenate(x, axis=0) for x in pieces)
    half = lax.broadcasted_iota(jnp.int32, real.shape, 1) < LANES // 2
    even = jnp.where(half, real, pltpu.roll(imag, LANES // 2, 1)).astype(jnp.bfloat16)
    odd = jnp.where(half, pltpu.roll(real, LANES // 2, 1), imag).astype(jnp.bfloat16)
    rows, _, mics = out_ref.shape[:3]
    for row in range(rows):
        for mic in range(mics):
            out_ref[row, 0, mic] = even
            out_ref[row, 1, mic] = odd


def spectra_of(table, time_data, devices):
    seg, mic, samples = time_data.shape
    lines = seg * mic // LANES
    return pl.pallas_call(
        spectra_kernel,
        out_shape=jax.ShapeDtypeStruct(devices + (lines, LANES), jnp.bfloat16),
        in_specs=[pl.BlockSpec(memory_space=pltpu.VMEM)] * 2,
        out_specs=pl.BlockSpec(memory_space=pltpu.VMEM),
        compiler_params=pltpu.CompilerParams(vmem_limit_bytes=16 * MIB),
        cost_estimate=pl.CostEstimate(
            flops=4 * time_data.size, bytes_accessed=2 * time_data.size, transcendentals=0
        ),
    )(table, time_data.reshape(seg * mic, samples))


def power_kernel(spec_ref, steer_ref, out_ref):
    groups, devices, segs, _ = spec_ref.shape
    width = out_ref.shape[1]
    half = lax.broadcasted_iota(jnp.int32, (segs, LANES), 1) < LANES // 2
    real, imag = [], []
    for g in range(groups):
        blocks = [spec_ref[g, d] for d in range(devices)]
        real.append(jnp.concatenate(blocks, axis=1))
        turned = [pltpu.roll(x, LANES // 2, 1) for x in blocks]
        imag.append(jnp.concatenate([jnp.where(half, x, -x) for x in turned], axis=1))
    left = jnp.concatenate(real + imag, axis=0)
    steering = steer_ref[...].reshape(left.shape[1], width)
    beams = jnp.dot(left, steering, preferred_element_type=jnp.float32)
    out_ref[...] = jnp.sum(beams * beams, axis=0, keepdims=True)


def power_of(spectra, steering):
    width = steering.shape[2]
    return pl.pallas_call(
        power_kernel,
        out_shape=jax.ShapeDtypeStruct((1, width), jnp.float32),
        in_specs=[pl.BlockSpec(memory_space=pltpu.VMEM)] * 2,
        out_specs=pl.BlockSpec(memory_space=pltpu.VMEM),
        compiler_params=pltpu.CompilerParams(vmem_limit_bytes=16 * MIB),
        cost_estimate=pl.CostEstimate(
            flops=2 * 128 * steering.size, bytes_accessed=2 * steering.size, transcendentals=0
        ),
    )(spectra, steering)


def last_kernel(own_ref, other_ref, out_ref, *, scale):
    out_ref[...] = (own_ref[...] + other_ref[...]) / jnp.float32(scale)


def last_of(own, other, scale):
    return pl.pallas_call(
        functools.partial(last_kernel, scale=scale),
        out_shape=jax.ShapeDtypeStruct(own.shape, jnp.float32),
        in_specs=[pl.BlockSpec(memory_space=pltpu.VMEM)] * 2,
        out_specs=pl.BlockSpec(memory_space=pltpu.VMEM),
        compiler_params=pltpu.CompilerParams(vmem_limit_bytes=16 * MIB),
        cost_estimate=pl.CostEstimate(flops=2 * own.size, bytes_accessed=12 * own.size, transcendentals=0),
    )(own, other)


def shards(time_data, order_bin, mic_pos, grid_pos):
    seg_dev, mic_dev, samples = time_data.shape
    rows = lax.axis_size("row")
    cores = lax.axis_size("core")
    seg_count = rows * cores
    mic_count = lax.axis_size("mic")
    own_width = grid_pos.shape[1] // seg_count
    denom = seg_count * seg_dev * mic_count * mic_dev * 0.375 * samples
    swap = [(0, 1), (1, 0)]
    first, order_bin = lax.optimization_barrier((lead(), order_bin))
    table, steering = setup_of(order_bin, first, mic_pos, grid_pos, mic_count // 2, own_width, samples)
    twin_steering = lax.ppermute(steering, "core", swap)
    every = spectra_of(table, time_data, (rows, cores, mic_count))
    every = every.reshape((seg_count * mic_count,) + every.shape[3:])
    every = lax.all_to_all(every, ("row", "core", "mic"), 0, 0, tiled=True)
    every = every.reshape((seg_count, mic_count) + every.shape[1:])
    others = lax.ppermute(power_of(every, twin_steering), "core", swap)
    return last_of(power_of(every, steering), others, denom)


def solution(mesh):
    seg_count, mic_count = mesh.shape["seg"], mesh.shape["mic"]
    split = jax.sharding.Mesh(
        mesh.devices.reshape(seg_count // 2, 2, mic_count), ("row", "core", "mic")
    )
    seg = ("row", "core")
    placed = (P(seg, "mic", None), P(), P(), P(None, "mic"))
    return jax.shard_map(
        shards, mesh=split, in_specs=placed, out_specs=P("mic", seg), check_vma=False
    )
```

```python
import functools

import jax
import jax.numpy as jnp
import numpy as np
from jax import lax
from jax.experimental import pallas as pl
from jax.experimental.pallas import tpu as pltpu
from jax.sharding import PartitionSpec as P

LANES = 128
MIB = 1024 * 1024


def fitted(values, degree):
    count = degree + 1
    nodes = 0.125 + 0.125 * np.cos((2 * np.arange(count) + 1) * np.pi / (2 * count))
    return [float(c) for c in np.linalg.solve(np.vander(nodes, count, increasing=True), values(nodes))]


COS_FIT = fitted(lambda q: np.cos(2 * np.pi * np.sqrt(q)), 6)
SIN_FIT = fitted(lambda q: np.sin(2 * np.pi * np.sqrt(q)) / np.sqrt(q), 5)


def horner(coefficients, q):
    total = q * coefficients[-1] + coefficients[-2]
    for c in coefficients[-3::-1]:
        total = total * q + c
    return total


def cos_sin_turns(turns):
    r = turns - jnp.round(turns)
    q = r * r
    return horner(COS_FIT, q), r * horner(SIN_FIT, q)


def window_kernel(out_ref):
    times = lax.broadcasted_iota(jnp.int32, out_ref.shape, 1)
    cos_w, _ = cos_sin_turns(times.astype(jnp.float32) * (1.0 / out_ref.shape[1]))
    out_ref[...] = 0.5 - 0.5 * cos_w


def window_of(samples):
    return pl.pallas_call(
        window_kernel,
        out_shape=jax.ShapeDtypeStruct((8, samples), jnp.float32),
        out_specs=pl.BlockSpec(memory_space=pltpu.VMEM),
        compiler_params=pltpu.CompilerParams(vmem_limit_bytes=16 * MIB),
        cost_estimate=pl.CostEstimate(flops=8 * 2**30, bytes_accessed=2**24, transcendentals=0),
    )()


def table_of(order, window):
    samples = window.shape[1]
    times = lax.broadcasted_iota(jnp.int32, window.shape, 1)
    row = lax.broadcasted_iota(jnp.int32, window.shape, 0)
    turned = lax.rem(order * times, jnp.int32(samples))
    cos_a, sin_a = cos_sin_turns(turned.astype(jnp.float32) * (1.0 / samples))
    table = jnp.where(row == 0, window * cos_a, jnp.where(row == 1, -(window * sin_a), 0.0))
    return table.astype(jnp.bfloat16)


def steer(order, samples, points, mic_ref, steer_ref, column, first_pair):
    per_mm = order.astype(jnp.float32) * jnp.float32(51200.0 / 343.0 / 1000.0 / samples)
    points = points * per_mm
    half = LANES // 2
    for k in range(steer_ref.shape[0]):
        pair = first_pair + k
        mics = mic_ref[:, pair * LANES : (pair + 1) * LANES].astype(jnp.float32) * per_mm
        mics = jnp.concatenate([mics, jnp.zeros((5, LANES), jnp.float32)], axis=0)
        column[...] = jnp.transpose(mics)
        for first in range(0, LANES, 16):
            mine = column[first : first + 16, :]
            square = None
            for axis in range(3):
                gap = points[axis : axis + 1, :] - mine[:, axis : axis + 1]
                square = gap * gap if square is None else square + gap * gap
            turns = square * lax.rsqrt(jnp.maximum(square, 1e-12))
            cosine, sine = cos_sin_turns(turns)
            row = first // half * LANES + first % half
            steer_ref[k, row : row + 16, :] = cosine.astype(jnp.bfloat16)
            steer_ref[k, row + half : row + half + 16, :] = (-sine).astype(jnp.bfloat16)


def own_points(grid_ref, width):
    offset = pl.multiple_of(lax.axis_index(("row", "core")) * width, width)
    return grid_ref[:, pl.ds(offset, width)].astype(jnp.float32)


def setup_kernel(order_ref, window_ref, mic_ref, grid_ref, table_ref, steer_ref, column, *, width):
    table_ref[...] = table_of(order_ref[0], window_ref[...])
    samples = table_ref.shape[1]
    steer(order_ref[0], samples, own_points(grid_ref, width), mic_ref, steer_ref, column, 0)


def setup_of(order_bin, window, mic_pos, grid_pos, pairs, width):
    samples = window.shape[1]
    return pl.pallas_call(
        functools.partial(setup_kernel, width=width),
        out_shape=[
            jax.ShapeDtypeStruct((8, samples), jnp.bfloat16),
            jax.ShapeDtypeStruct((pairs, 2 * LANES, width), jnp.bfloat16),
        ],
        in_specs=[pl.BlockSpec(memory_space=pltpu.SMEM)] + [pl.BlockSpec(memory_space=pltpu.VMEM)] * 3,
        out_specs=[pl.BlockSpec(memory_space=pltpu.VMEM)] * 2,
        scratch_shapes=[pltpu.VMEM((LANES, 8), jnp.float32)],
        compiler_params=pltpu.CompilerParams(vmem_limit_bytes=16 * MIB),
        cost_estimate=pl.CostEstimate(flops=2 * 2**30, bytes_accessed=2**22, transcendentals=0),
    )(order_bin, window, mic_pos, grid_pos)


def spectra_kernel(table_ref, data_ref, out_ref):
    samples = data_ref.shape[1]
    lines = data_ref.shape[0] // LANES
    shares = (4, 4)
    table = table_ref[...]
    wide = table.astype(jnp.float32)
    factors = [
        [jnp.broadcast_to(wide[part : part + 1, c : c + LANES], (LANES, LANES)) for c in range(0, samples, LANES)]
        for part in range(2)
    ]
    pieces = ([], [])
    for first in range(0, lines, sum(shares)):
        block = data_ref[pl.ds(first * LANES, shares[0] * LANES)]
        spec = lax.dot_general(
            table, block, (((1,), (1,)), ((), ())), preferred_element_type=jnp.float32
        )
        for part in range(2):
            pieces[part].extend(spec[part : part + 1, j * LANES : (j + 1) * LANES] for j in range(shares[0]))
        for line in range(first + shares[0], first + sum(shares)):
            sums = [None, None]
            for c in range(samples // LANES):
                rows = data_ref[pl.ds(line * LANES, LANES), pl.ds(c * LANES, LANES)].astype(jnp.float32)
                for part in range(2):
                    term = rows * factors[part][c]
                    sums[part] = term if sums[part] is None else sums[part] + term
            for part in range(2):
                turned = jnp.transpose(sums[part])
                pieces[part].append(jnp.sum(turned, axis=0, keepdims=True))
    real, imag = (jnp.concatenate(x, axis=0) for x in pieces)
    half = lax.broadcasted_iota(jnp.int32, real.shape, 1) < LANES // 2
    even = jnp.where(half, real, pltpu.roll(imag, LANES // 2, 1)).astype(jnp.bfloat16)
    odd = jnp.where(half, pltpu.roll(real, LANES // 2, 1), imag).astype(jnp.bfloat16)
    rows, _, mics = out_ref.shape[:3]
    for row in range(rows):
        for mic in range(mics):
            out_ref[row, 0, mic] = even
            out_ref[row, 1, mic] = odd


def spectra_of(table, time_data, devices):
    seg, mic, samples = time_data.shape
    lines = seg * mic // LANES
    return pl.pallas_call(
        spectra_kernel,
        out_shape=jax.ShapeDtypeStruct(devices + (lines, LANES), jnp.bfloat16),
        in_specs=[pl.BlockSpec(memory_space=pltpu.VMEM)] * 2,
        out_specs=pl.BlockSpec(memory_space=pltpu.VMEM),
        compiler_params=pltpu.CompilerParams(vmem_limit_bytes=16 * MIB),
        cost_estimate=pl.CostEstimate(
            flops=4 * time_data.size, bytes_accessed=2 * time_data.size, transcendentals=0
        ),
    )(table, time_data.reshape(seg * mic, samples))


def steering_kernel(order_ref, mic_ref, grid_ref, out_ref, column, *, first_pair, samples, width):
    steer(order_ref[0], samples, own_points(grid_ref, width), mic_ref, out_ref, column, first_pair)


def steering_of(order_bin, mic_pos, grid_pos, first_pair, samples, width):
    pairs = mic_pos.shape[1] // LANES - first_pair
    return pl.pallas_call(
        functools.partial(steering_kernel, first_pair=first_pair, samples=samples, width=width),
        out_shape=jax.ShapeDtypeStruct((pairs, 2 * LANES, width), jnp.bfloat16),
        in_specs=[pl.BlockSpec(memory_space=pltpu.SMEM)] + [pl.BlockSpec(memory_space=pltpu.VMEM)] * 2,
        out_specs=pl.BlockSpec(memory_space=pltpu.VMEM),
        scratch_shapes=[pltpu.VMEM((LANES, 8), jnp.float32)],
        compiler_params=pltpu.CompilerParams(vmem_limit_bytes=16 * MIB),
        cost_estimate=pl.CostEstimate(
            flops=50 * pairs * LANES * width, bytes_accessed=4 * pairs * LANES * width, transcendentals=0
        ),
    )(order_bin, mic_pos, grid_pos)


def power_kernel(spec_ref, steer_a_ref, steer_b_ref, before_ref, out_ref, *, scale):
    groups, devices, segs, _ = spec_ref.shape
    width = out_ref.shape[1]
    half = lax.broadcasted_iota(jnp.int32, (segs, LANES), 1) < LANES // 2
    real, imag = [], []
    for g in range(groups):
        blocks = [spec_ref[g, d] for d in range(devices)]
        real.append(jnp.concatenate(blocks, axis=1))
        turned = [pltpu.roll(x, LANES // 2, 1) for x in blocks]
        imag.append(jnp.concatenate([jnp.where(half, x, -x) for x in turned], axis=1))
    left = jnp.concatenate(real + imag, axis=0)
    beams = None
    start = 0
    for ref in (steer_a_ref, steer_b_ref):
        depth = ref.shape[0] * ref.shape[1]
        term = jnp.dot(
            left[:, start : start + depth], ref[...].reshape(depth, width), preferred_element_type=jnp.float32
        )
        beams = term if beams is None else beams + term
        start += depth
    power = jnp.sum((beams * beams).reshape(-1, 8, width), axis=0) + before_ref[...]
    if scale is None:
        out_ref[...] = power
    else:
        out_ref[...] = jnp.sum(power, axis=0, keepdims=True) / jnp.float32(scale)


def power_of(spectra, steering, before, scale):
    width = steering[0].shape[2]
    size = 2 * steering[0].size
    shape = (8 if scale is None else 1, width)
    return pl.pallas_call(
        functools.partial(power_kernel, scale=scale),
        out_shape=jax.ShapeDtypeStruct(shape, jnp.float32),
        in_specs=[pl.BlockSpec(memory_space=pltpu.VMEM)] * 4,
        out_specs=pl.BlockSpec(memory_space=pltpu.VMEM),
        compiler_params=pltpu.CompilerParams(vmem_limit_bytes=16 * MIB),
        cost_estimate=pl.CostEstimate(
            flops=2 * 128 * size, bytes_accessed=2 * size, transcendentals=0
        ),
    )(spectra, *steering, before)


def shards(time_data, order_bin, mic_pos, grid_pos):
    seg_dev, mic_dev, samples = time_data.shape
    rows = lax.axis_size("row")
    cores = lax.axis_size("core")
    seg_count = rows * cores
    mic_count = lax.axis_size("mic")
    own_width = grid_pos.shape[1] // seg_count
    denom = seg_count * seg_dev * mic_count * mic_dev * 0.375 * samples
    early = mic_count // 4
    window, order_bin = lax.optimization_barrier((window_of(samples), order_bin))
    table, steering_a = setup_of(order_bin, window, mic_pos, grid_pos, early, own_width)
    every = spectra_of(table, time_data, (rows, cores, mic_count))
    every = every.reshape((seg_count * mic_count,) + every.shape[3:])
    every = lax.all_to_all(every, ("row", "core", "mic"), 0, 0, tiled=True)
    twin = lax.ppermute(every, "core", [(0, 1), (1, 0)])
    every, later_order = lax.optimization_barrier((every, order_bin))
    steering = (steering_a, steering_of(later_order, mic_pos, grid_pos, early, samples, own_width))
    shape = (seg_count, mic_count) + every.shape[1:]
    half = power_of(every.reshape(shape), steering, jnp.zeros((8, own_width), jnp.float32), None)
    return power_of(twin.reshape(shape), steering, half, denom)


def solution(mesh):
    seg_count, mic_count = mesh.shape["seg"], mesh.shape["mic"]
    split = jax.sharding.Mesh(
        mesh.devices.reshape(seg_count // 2, 2, mic_count), ("row", "core", "mic")
    )
    seg = ("row", "core")
    placed = (P(seg, "mic", None), P(), P(), P(None, "mic"))
    return jax.shard_map(
        shards, mesh=split, in_specs=placed, out_specs=P("mic", seg), check_vma=False
    )
```

```python
import functools

import jax
import jax.numpy as jnp
import numpy as np
from jax import lax
from jax.experimental import pallas as pl
from jax.experimental.pallas import tpu as pltpu
from jax.sharding import PartitionSpec as P

LANES = 128
MIB = 1024 * 1024
NEAREST = 1.5 * 2.0**23


def fitted(values, degree):
    count = degree + 1
    nodes = 0.125 + 0.125 * np.cos((2 * np.arange(count) + 1) * np.pi / (2 * count))
    return [float(c) for c in np.linalg.solve(np.vander(nodes, count, increasing=True), values(nodes))]


COS_FIT = fitted(lambda q: np.cos(2 * np.pi * np.sqrt(q)), 6)
SIN_FIT = fitted(lambda q: np.sin(2 * np.pi * np.sqrt(q)) / np.sqrt(q), 5)


def horner(coefficients, q):
    total = q * coefficients[-1] + coefficients[-2]
    for c in coefficients[-3::-1]:
        total = total * q + c
    return total


def cos_sin_turns(turns):
    r = turns - ((turns + NEAREST) - NEAREST)
    q = r * r
    return horner(COS_FIT, q), r * horner(SIN_FIT, q)


def window_kernel(out_ref):
    times = lax.broadcasted_iota(jnp.int32, out_ref.shape, 1)
    cos_w, _ = cos_sin_turns(times.astype(jnp.float32) * (1.0 / out_ref.shape[1]))
    out_ref[...] = 0.5 - 0.5 * cos_w


def window_of(samples):
    return pl.pallas_call(
        window_kernel,
        out_shape=jax.ShapeDtypeStruct((8, samples), jnp.float32),
        out_specs=pl.BlockSpec(memory_space=pltpu.VMEM),
        compiler_params=pltpu.CompilerParams(vmem_limit_bytes=16 * MIB),
        cost_estimate=pl.CostEstimate(flops=8 * 2**30, bytes_accessed=2**24, transcendentals=0),
    )()


def table_of(order, window):
    samples = window.shape[1]
    times = lax.broadcasted_iota(jnp.int32, window.shape, 1)
    row = lax.broadcasted_iota(jnp.int32, window.shape, 0)
    turned = lax.rem(order * times, jnp.int32(samples))
    cos_a, sin_a = cos_sin_turns(turned.astype(jnp.float32) * (1.0 / samples))
    table = jnp.where(row == 0, window * cos_a, jnp.where(row == 1, -(window * sin_a), 0.0))
    return table.astype(jnp.bfloat16)


def steer(order, samples, points, mic_ref, steer_ref, column, first_pair):
    per_mm = order.astype(jnp.float32) * jnp.float32(51200.0 / 343.0 / 1000.0 / samples)
    half = LANES // 2
    for k in range(steer_ref.shape[0]):
        pair = first_pair + k
        mics = mic_ref[:, pair * LANES : (pair + 1) * LANES].astype(jnp.float32)
        mics = jnp.concatenate([mics, jnp.zeros((5, LANES), jnp.float32)], axis=0)
        column[...] = jnp.transpose(mics)
        for first in range(0, LANES, 16):
            mine = column[first : first + 16, :]
            square = None
            for axis in range(3):
                gap = points[axis : axis + 1, :] - mine[:, axis : axis + 1]
                square = gap * gap if square is None else square + gap * gap
            turns = square * lax.rsqrt(jnp.maximum(square, 1.0)) * per_mm
            cosine, sine = cos_sin_turns(turns)
            row = first // half * LANES + first % half
            steer_ref[k, row : row + 16, :] = cosine.astype(jnp.bfloat16)
            steer_ref[k, row + half : row + half + 16, :] = (-sine).astype(jnp.bfloat16)


def own_points(grid_ref, width):
    offset = pl.multiple_of(lax.axis_index(("row", "core")) * width, width)
    return grid_ref[:, pl.ds(offset, width)].astype(jnp.float32)


def setup_kernel(
    order_ref, window_ref, mic_ref, grid_ref, table_ref, wide_ref, steer_ref, column, *, width
):
    table = table_of(order_ref[0], window_ref[...])
    table_ref[...] = table
    for part in range(2):
        row = table[part : part + 1].astype(jnp.float32)
        wide_ref[part] = jnp.broadcast_to(row, wide_ref.shape[1:])
    samples = table_ref.shape[1]
    steer(order_ref[0], samples, own_points(grid_ref, width), mic_ref, steer_ref, column, 0)


def setup_of(order_bin, window, mic_pos, grid_pos, pairs, width):
    samples = window.shape[1]
    return pl.pallas_call(
        functools.partial(setup_kernel, width=width),
        out_shape=[
            jax.ShapeDtypeStruct((8, samples), jnp.bfloat16),
            jax.ShapeDtypeStruct((2, 8, samples), jnp.float32),
            jax.ShapeDtypeStruct((pairs, 2 * LANES, width), jnp.bfloat16),
        ],
        in_specs=[pl.BlockSpec(memory_space=pltpu.SMEM)] + [pl.BlockSpec(memory_space=pltpu.VMEM)] * 3,
        out_specs=[pl.BlockSpec(memory_space=pltpu.VMEM)] * 3,
        scratch_shapes=[pltpu.VMEM((LANES, 8), jnp.float32)],
        compiler_params=pltpu.CompilerParams(vmem_limit_bytes=16 * MIB),
        cost_estimate=pl.CostEstimate(flops=2 * 2**30, bytes_accessed=2**22, transcendentals=0),
    )(order_bin, window, mic_pos, grid_pos)


def spectra_kernel(table_ref, wide_ref, data_ref, out_ref):
    samples = data_ref.shape[1]
    lines = data_ref.shape[0] // LANES
    shares = (4, 4)
    table = table_ref[...]
    pieces = ([], [])
    for first in range(0, lines, sum(shares)):
        block = data_ref[pl.ds(first * LANES, shares[0] * LANES)]
        spec = lax.dot_general(
            table, block, (((1,), (1,)), ((), ())), preferred_element_type=jnp.float32
        )
        for part in range(2):
            pieces[part].extend(spec[part : part + 1, j * LANES : (j + 1) * LANES] for j in range(shares[0]))
        for line in range(first + shares[0], first + sum(shares)):
            sums = [None, None]
            for c in range(samples // LANES):
                rows = data_ref[pl.ds(line * LANES, LANES), pl.ds(c * LANES, LANES)].astype(jnp.float32)
                rows = rows.reshape(-1, 8, LANES)
                for part in range(2):
                    term = rows * wide_ref[part, :, c * LANES : (c + 1) * LANES]
                    sums[part] = term if sums[part] is None else sums[part] + term
            for part in range(2):
                turned = jnp.transpose(sums[part].reshape(LANES, LANES))
                pieces[part].append(jnp.sum(turned, axis=0, keepdims=True))
    real, imag = (jnp.concatenate(x, axis=0) for x in pieces)
    half = lax.broadcasted_iota(jnp.int32, real.shape, 1) < LANES // 2
    even = jnp.where(half, real, pltpu.roll(imag, LANES // 2, 1)).astype(jnp.bfloat16)
    odd = jnp.where(half, pltpu.roll(real, LANES // 2, 1), imag).astype(jnp.bfloat16)
    rows, _, mics = out_ref.shape[:3]
    for row in range(rows):
        for mic in range(mics):
            out_ref[row, 0, mic] = even
            out_ref[row, 1, mic] = odd


def spectra_of(table, wide, time_data, devices):
    seg, mic, samples = time_data.shape
    lines = seg * mic // LANES
    return pl.pallas_call(
        spectra_kernel,
        out_shape=jax.ShapeDtypeStruct(devices + (lines, LANES), jnp.bfloat16),
        in_specs=[pl.BlockSpec(memory_space=pltpu.VMEM)] * 3,
        out_specs=pl.BlockSpec(memory_space=pltpu.VMEM),
        compiler_params=pltpu.CompilerParams(vmem_limit_bytes=16 * MIB),
        cost_estimate=pl.CostEstimate(
            flops=4 * time_data.size, bytes_accessed=2 * time_data.size, transcendentals=0
        ),
    )(table, wide, time_data.reshape(seg * mic, samples))


def steering_kernel(order_ref, mic_ref, grid_ref, out_ref, column, *, first_pair, samples, width):
    steer(order_ref[0], samples, own_points(grid_ref, width), mic_ref, out_ref, column, first_pair)


def steering_of(order_bin, mic_pos, grid_pos, first_pair, samples, width):
    pairs = mic_pos.shape[1] // LANES - first_pair
    return pl.pallas_call(
        functools.partial(steering_kernel, first_pair=first_pair, samples=samples, width=width),
        out_shape=jax.ShapeDtypeStruct((pairs, 2 * LANES, width), jnp.bfloat16),
        in_specs=[pl.BlockSpec(memory_space=pltpu.SMEM)] + [pl.BlockSpec(memory_space=pltpu.VMEM)] * 2,
        out_specs=pl.BlockSpec(memory_space=pltpu.VMEM),
        scratch_shapes=[pltpu.VMEM((LANES, 8), jnp.float32)],
        compiler_params=pltpu.CompilerParams(vmem_limit_bytes=16 * MIB),
        cost_estimate=pl.CostEstimate(
            flops=50 * pairs * LANES * width, bytes_accessed=4 * pairs * LANES * width, transcendentals=0
        ),
    )(order_bin, mic_pos, grid_pos)


def power_kernel(spec_ref, steer_a_ref, steer_b_ref, before_ref, out_ref, *, scale):
    groups, devices, segs, _ = spec_ref.shape
    width = out_ref.shape[1]
    half = lax.broadcasted_iota(jnp.int32, (segs, LANES), 1) < LANES // 2
    real, imag = [], []
    for g in range(groups):
        blocks = [spec_ref[g, d] for d in range(devices)]
        real.append(jnp.concatenate(blocks, axis=1))
        turned = [pltpu.roll(x, LANES // 2, 1) for x in blocks]
        imag.append(jnp.concatenate([jnp.where(half, x, -x) for x in turned], axis=1))
    left = jnp.concatenate(real + imag, axis=0)
    beams = None
    start = 0
    for ref in (steer_a_ref, steer_b_ref):
        depth = ref.shape[0] * ref.shape[1]
        term = jnp.dot(
            left[:, start : start + depth], ref[...].reshape(depth, width), preferred_element_type=jnp.float32
        )
        beams = term if beams is None else beams + term
        start += depth
    power = jnp.sum((beams * beams).reshape(-1, 8, width), axis=0) + before_ref[...]
    if scale is None:
        out_ref[...] = power
    else:
        out_ref[...] = jnp.sum(power, axis=0, keepdims=True) / jnp.float32(scale)


def power_of(spectra, steering, before, scale):
    width = steering[0].shape[2]
    size = 2 * steering[0].size
    shape = (8 if scale is None else 1, width)
    return pl.pallas_call(
        functools.partial(power_kernel, scale=scale),
        out_shape=jax.ShapeDtypeStruct(shape, jnp.float32),
        in_specs=[pl.BlockSpec(memory_space=pltpu.VMEM)] * 4,
        out_specs=pl.BlockSpec(memory_space=pltpu.VMEM),
        compiler_params=pltpu.CompilerParams(vmem_limit_bytes=16 * MIB),
        cost_estimate=pl.CostEstimate(
            flops=2 * 128 * size, bytes_accessed=2 * size, transcendentals=0
        ),
    )(spectra, *steering, before)


def shards(time_data, order_bin, mic_pos, grid_pos):
    seg_dev, mic_dev, samples = time_data.shape
    rows = lax.axis_size("row")
    cores = lax.axis_size("core")
    seg_count = rows * cores
    mic_count = lax.axis_size("mic")
    own_width = grid_pos.shape[1] // seg_count
    denom = seg_count * seg_dev * mic_count * mic_dev * 0.375 * samples
    early = 3 * (mic_count // 2) // 4
    window, order_bin = lax.optimization_barrier((window_of(samples), order_bin))
    table, wide, steering_a = setup_of(order_bin, window, mic_pos, grid_pos, early, own_width)
    every = spectra_of(table, wide, time_data, (rows, cores, mic_count))
    every = every.reshape((seg_count * mic_count,) + every.shape[3:])
    every = lax.all_to_all(every, ("row", "core", "mic"), 0, 0, tiled=True)
    twin = lax.ppermute(every, "core", [(0, 1), (1, 0)])
    every, later_order = lax.optimization_barrier((every, order_bin))
    steering = (steering_a, steering_of(later_order, mic_pos, grid_pos, early, samples, own_width))
    shape = (seg_count, mic_count) + every.shape[1:]
    half = power_of(every.reshape(shape), steering, jnp.zeros((8, own_width), jnp.float32), None)
    return power_of(twin.reshape(shape), steering, half, denom)


def solution(mesh):
    seg_count, mic_count = mesh.shape["seg"], mesh.shape["mic"]
    split = jax.sharding.Mesh(
        mesh.devices.reshape(seg_count // 2, 2, mic_count), ("row", "core", "mic")
    )
    seg = ("row", "core")
    placed = (P(seg, "mic", None), P(), P(), P(None, "mic"))
    return jax.shard_map(
        shards, mesh=split, in_specs=placed, out_specs=P("mic", seg), check_vma=False
    )
```

```python
import functools

import jax
import jax.numpy as jnp
import numpy as np
from jax import lax
from jax.experimental import pallas as pl
from jax.experimental.pallas import tpu as pltpu
from jax.sharding import PartitionSpec as P

LANES = 128
MIB = 1024 * 1024
NEAREST = 1.5 * 2.0**23


def fitted(values, degree):
    count = degree + 1
    nodes = 0.125 + 0.125 * np.cos((2 * np.arange(count) + 1) * np.pi / (2 * count))
    return [float(c) for c in np.linalg.solve(np.vander(nodes, count, increasing=True), values(nodes))]


COS_FIT = fitted(lambda q: np.cos(2 * np.pi * np.sqrt(q)), 6)
SIN_FIT = fitted(lambda q: np.sin(2 * np.pi * np.sqrt(q)) / np.sqrt(q), 5)


def horner(coefficients, q):
    total = q * coefficients[-1] + coefficients[-2]
    for c in coefficients[-3::-1]:
        total = total * q + c
    return total


def cos_sin_turns(turns):
    r = turns - ((turns + NEAREST) - NEAREST)
    q = r * r
    return horner(COS_FIT, q), r * horner(SIN_FIT, q)


def window_kernel(out_ref):
    times = lax.broadcasted_iota(jnp.int32, out_ref.shape, 1)
    cos_w, _ = cos_sin_turns(times.astype(jnp.float32) * (1.0 / out_ref.shape[1]))
    out_ref[...] = 0.5 - 0.5 * cos_w


def window_of(samples):
    return pl.pallas_call(
        window_kernel,
        out_shape=jax.ShapeDtypeStruct((8, samples), jnp.float32),
        out_specs=pl.BlockSpec(memory_space=pltpu.VMEM),
        compiler_params=pltpu.CompilerParams(vmem_limit_bytes=16 * MIB),
        cost_estimate=pl.CostEstimate(flops=8 * 2**30, bytes_accessed=2**24, transcendentals=0),
    )()


def table_of(order, window):
    samples = window.shape[1]
    times = lax.broadcasted_iota(jnp.int32, window.shape, 1)
    row = lax.broadcasted_iota(jnp.int32, window.shape, 0)
    turned = lax.rem(order * times, jnp.int32(samples))
    cos_a, sin_a = cos_sin_turns(turned.astype(jnp.float32) * (1.0 / samples))
    table = jnp.where(row == 0, window * cos_a, jnp.where(row == 1, -(window * sin_a), 0.0))
    return table.astype(jnp.bfloat16)


def steer(order, samples, points, mic_ref, steer_ref, column, first_pair):
    per_mm = order.astype(jnp.float32) * jnp.float32(51200.0 / 343.0 / 1000.0 / samples)
    half = LANES // 2
    for k in range(steer_ref.shape[0]):
        pair = first_pair + k
        mics = mic_ref[:, pair * LANES : (pair + 1) * LANES].astype(jnp.float32)
        mics = jnp.concatenate([mics, jnp.zeros((5, LANES), jnp.float32)], axis=0)
        column[...] = jnp.transpose(mics)
        for first in range(0, LANES, 16):
            mine = column[first : first + 16, :]
            square = None
            for axis in range(3):
                gap = points[axis : axis + 1, :] - mine[:, axis : axis + 1]
                square = gap * gap if square is None else square + gap * gap
            turns = square * lax.rsqrt(jnp.maximum(square, 1.0)) * per_mm
            cosine, sine = cos_sin_turns(turns)
            row = first // half * LANES + first % half
            steer_ref[k, row : row + 16, :] = cosine.astype(jnp.bfloat16)
            steer_ref[k, row + half : row + half + 16, :] = (-sine).astype(jnp.bfloat16)


def own_points(grid_ref, width):
    offset = pl.multiple_of(lax.axis_index(("row", "core")) * width, width)
    return grid_ref[:, pl.ds(offset, width)].astype(jnp.float32)


def setup_kernel(
    order_ref, window_ref, mic_ref, grid_ref, table_ref, wide_ref, steer_ref, column, *, width
):
    table = table_of(order_ref[0], window_ref[...])
    table_ref[...] = table
    for part in range(2):
        row = table[part : part + 1].astype(jnp.float32)
        wide_ref[part] = jnp.broadcast_to(row, wide_ref.shape[1:])
    samples = table_ref.shape[1]
    steer(order_ref[0], samples, own_points(grid_ref, width), mic_ref, steer_ref, column, 0)


def setup_of(order_bin, window, mic_pos, grid_pos, pairs, width):
    samples = window.shape[1]
    return pl.pallas_call(
        functools.partial(setup_kernel, width=width),
        out_shape=[
            jax.ShapeDtypeStruct((8, samples), jnp.bfloat16),
            jax.ShapeDtypeStruct((2, 8, samples), jnp.float32),
            jax.ShapeDtypeStruct((pairs, 2 * LANES, width), jnp.bfloat16),
        ],
        in_specs=[pl.BlockSpec(memory_space=pltpu.SMEM)] + [pl.BlockSpec(memory_space=pltpu.VMEM)] * 3,
        out_specs=[pl.BlockSpec(memory_space=pltpu.VMEM)] * 3,
        scratch_shapes=[pltpu.VMEM((LANES, 8), jnp.float32)],
        compiler_params=pltpu.CompilerParams(vmem_limit_bytes=16 * MIB),
        cost_estimate=pl.CostEstimate(flops=2 * 2**30, bytes_accessed=2**22, transcendentals=0),
    )(order_bin, window, mic_pos, grid_pos)


def spectra_kernel(table_ref, wide_ref, data_ref, out_ref):
    samples = data_ref.shape[1]
    lines = data_ref.shape[0] // LANES
    shares = (5, 3)
    table = table_ref[...]
    pieces = ([], [])
    for first in range(0, lines, sum(shares)):
        block = data_ref[pl.ds(first * LANES, shares[0] * LANES)]
        spec = lax.dot_general(
            table, block, (((1,), (1,)), ((), ())), preferred_element_type=jnp.float32
        )
        for part in range(2):
            pieces[part].extend(spec[part : part + 1, j * LANES : (j + 1) * LANES] for j in range(shares[0]))
        for line in range(first + shares[0], first + sum(shares)):
            sums = [None, None]
            for c in range(samples // LANES):
                rows = data_ref[pl.ds(line * LANES, LANES), pl.ds(c * LANES, LANES)].astype(jnp.float32)
                rows = rows.reshape(-1, 8, LANES)
                for part in range(2):
                    term = rows * wide_ref[part, :, c * LANES : (c + 1) * LANES]
                    sums[part] = term if sums[part] is None else sums[part] + term
            for part in range(2):
                turned = jnp.transpose(sums[part].reshape(LANES, LANES))
                pieces[part].append(jnp.sum(turned, axis=0, keepdims=True))
    real, imag = (jnp.concatenate(x, axis=0) for x in pieces)
    half = lax.broadcasted_iota(jnp.int32, real.shape, 1) < LANES // 2
    even = jnp.where(half, real, pltpu.roll(imag, LANES // 2, 1)).astype(jnp.bfloat16)
    odd = jnp.where(half, pltpu.roll(real, LANES // 2, 1), imag).astype(jnp.bfloat16)
    rows, _, mics = out_ref.shape[:3]
    for row in range(rows):
        for mic in range(mics):
            out_ref[row, 0, mic] = even
            out_ref[row, 1, mic] = odd


def spectra_of(table, wide, time_data, devices):
    seg, mic, samples = time_data.shape
    lines = seg * mic // LANES
    return pl.pallas_call(
        spectra_kernel,
        out_shape=jax.ShapeDtypeStruct(devices + (lines, LANES), jnp.bfloat16),
        in_specs=[pl.BlockSpec(memory_space=pltpu.VMEM)] * 3,
        out_specs=pl.BlockSpec(memory_space=pltpu.VMEM),
        compiler_params=pltpu.CompilerParams(vmem_limit_bytes=16 * MIB),
        cost_estimate=pl.CostEstimate(
            flops=4 * time_data.size, bytes_accessed=2 * time_data.size, transcendentals=0
        ),
    )(table, wide, time_data.reshape(seg * mic, samples))


def steering_kernel(order_ref, mic_ref, grid_ref, out_ref, column, *, first_pair, samples, width):
    steer(order_ref[0], samples, own_points(grid_ref, width), mic_ref, out_ref, column, first_pair)


def steering_of(order_bin, mic_pos, grid_pos, first_pair, samples, width):
    pairs = mic_pos.shape[1] // LANES - first_pair
    return pl.pallas_call(
        functools.partial(steering_kernel, first_pair=first_pair, samples=samples, width=width),
        out_shape=jax.ShapeDtypeStruct((pairs, 2 * LANES, width), jnp.bfloat16),
        in_specs=[pl.BlockSpec(memory_space=pltpu.SMEM)] + [pl.BlockSpec(memory_space=pltpu.VMEM)] * 2,
        out_specs=pl.BlockSpec(memory_space=pltpu.VMEM),
        scratch_shapes=[pltpu.VMEM((LANES, 8), jnp.float32)],
        compiler_params=pltpu.CompilerParams(vmem_limit_bytes=16 * MIB),
        cost_estimate=pl.CostEstimate(
            flops=50 * pairs * LANES * width, bytes_accessed=4 * pairs * LANES * width, transcendentals=0
        ),
    )(order_bin, mic_pos, grid_pos)


def power_kernel(spec_ref, steer_a_ref, steer_b_ref, before_ref, out_ref, *, scale):
    groups, devices, segs, _ = spec_ref.shape
    width = out_ref.shape[1]
    half = lax.broadcasted_iota(jnp.int32, (segs, LANES), 1) < LANES // 2
    real, imag = [], []
    for g in range(groups):
        blocks = [spec_ref[g, d] for d in range(devices)]
        real.append(jnp.concatenate(blocks, axis=1))
        turned = [pltpu.roll(x, LANES // 2, 1) for x in blocks]
        imag.append(jnp.concatenate([jnp.where(half, x, -x) for x in turned], axis=1))
    left = jnp.concatenate(real + imag, axis=0)
    beams = None
    start = 0
    for ref in (steer_a_ref, steer_b_ref):
        depth = ref.shape[0] * ref.shape[1]
        term = jnp.dot(
            left[:, start : start + depth], ref[...].reshape(depth, width), preferred_element_type=jnp.float32
        )
        beams = term if beams is None else beams + term
        start += depth
    power = jnp.sum((beams * beams).reshape(-1, 8, width), axis=0) + before_ref[...]
    if scale is None:
        out_ref[...] = power
    else:
        out_ref[...] = jnp.sum(power, axis=0, keepdims=True) / jnp.float32(scale)


def power_of(spectra, steering, before, scale):
    width = steering[0].shape[2]
    size = 2 * steering[0].size
    shape = (8 if scale is None else 1, width)
    return pl.pallas_call(
        functools.partial(power_kernel, scale=scale),
        out_shape=jax.ShapeDtypeStruct(shape, jnp.float32),
        in_specs=[pl.BlockSpec(memory_space=pltpu.VMEM)] * 4,
        out_specs=pl.BlockSpec(memory_space=pltpu.VMEM),
        compiler_params=pltpu.CompilerParams(vmem_limit_bytes=16 * MIB),
        cost_estimate=pl.CostEstimate(
            flops=2 * 128 * size, bytes_accessed=2 * size, transcendentals=0
        ),
    )(spectra, *steering, before)


def shards(time_data, order_bin, mic_pos, grid_pos):
    seg_dev, mic_dev, samples = time_data.shape
    rows = lax.axis_size("row")
    cores = lax.axis_size("core")
    seg_count = rows * cores
    mic_count = lax.axis_size("mic")
    own_width = grid_pos.shape[1] // seg_count
    denom = seg_count * seg_dev * mic_count * mic_dev * 0.375 * samples
    early = 3 * (mic_count // 2) // 4
    window, order_bin = lax.optimization_barrier((window_of(samples), order_bin))
    table, wide, steering_a = setup_of(order_bin, window, mic_pos, grid_pos, early, own_width)
    every = spectra_of(table, wide, time_data, (rows, cores, mic_count))
    every = every.reshape((seg_count * mic_count,) + every.shape[3:])
    every = lax.all_to_all(every, ("row", "core", "mic"), 0, 0, tiled=True)
    twin = lax.ppermute(every, "core", [(0, 1), (1, 0)])
    every, later_order = lax.optimization_barrier((every, order_bin))
    steering = (steering_a, steering_of(later_order, mic_pos, grid_pos, early, samples, own_width))
    shape = (seg_count, mic_count) + every.shape[1:]
    half = power_of(every.reshape(shape), steering, jnp.zeros((8, own_width), jnp.float32), None)
    return power_of(twin.reshape(shape), steering, half, denom)


def solution(mesh):
    seg_count, mic_count = mesh.shape["seg"], mesh.shape["mic"]
    split = jax.sharding.Mesh(
        mesh.devices.reshape(seg_count // 2, 2, mic_count), ("row", "core", "mic")
    )
    seg = ("row", "core")
    placed = (P(seg, "mic", None), P(), P(), P(None, "mic"))
    return jax.shard_map(
        shards, mesh=split, in_specs=placed, out_specs=P("mic", seg), check_vma=False
    )
```
